32 devices in a mesh: groups: 2 (over x), hid: 8 (over z, y), mdl: 2 (over core).
Axes of the slice: x: 2, y: 2, z: 4, core: 2. Of those that a mesh axis runs over, the one named last changes fastest.
Arguments:
- tokens_q: bfloat16 [2, 512, 9216], P(None, 'groups', ('mdl', 'hid')), parts along dimension 1, may hold values from -6 to 6
- token_scale: float32 [2, 512], P(None, 'groups'), parts along dimension 1, may hold values from 0.5 to 4
- weight_in: bfloat16 [9216, 36864], P('mdl', 'hid'), may hold values from -0.0625 to 0.0625
- weight_out: bfloat16 [36864, 9216], P('hid', 'mdl'), may hold values from -0.046875 to 0.046875
Outputs:
- output_q: bfloat16 [2, 512, 9216], P(None, 'groups', ('mdl', 'hid')), parts along dimension 1
- output_scale: float32 [2, 512], P(None, 'groups'), parts along dimension 1
The draws below stay inside these ranges and needn't reach their ends.
There are 2 independent parts, one for each index of `groups`. The reference program is written for one: setup_inputs(seed, part) draws one part's arguments, and reference() takes and returns one part's arrays. A program takes and returns all parts, laid end to end along the dimension named above; an argument that names none is the same for every part. Nothing has to cross between parts.
All inputs are finite; a program needn't handle non-finite values. Where the reference program divides by a largest or mean magnitude, that divisor is 1e-20 or more.
Results may differ from the reference program's by a relative error of at most 0.005.
Values may be sent and summed in bfloat16 or wider, within the bound.
No kernel may reach another device: no remote copies, remote signals or barrier semaphores. Data moves between devices by JAX's collectives and lax.ppermute only.
A program may use at most 256 MiB of HBM per device.

```python
import math
import jax
import jax.numpy as jnp

D = 9216
FF = 36864
TOK = 256
STEPS = 2


def spiked(result, rng, source, target, blocks, factor):
    def block_of(axis_at):
        return (jnp.arange(result.shape[axis_at]) // (result.shape[axis_at] // blocks)).reshape((-1,) + (1,) * (result.ndim - 1 - axis_at))

    one_side = jax.random.permutation(rng, blocks)[block_of(target)]
    other_side = (block_of(target) + blocks // 2) % blocks
    return jnp.where((block_of(source) == one_side) | (block_of(source) == other_side), factor * result, result)


def block_scale(key, dims, cuts, least, high):
    factor_of, own = 1.0, jax.random.fold_in(key, 6)
    for dim, blocks in cuts:
        heights = jnp.exp(jax.random.uniform(jax.random.fold_in(own, dim), (blocks,), jnp.float32, least / len(cuts), high / len(cuts)))
        factor_of = factor_of * jnp.repeat(heights, dims[dim] // blocks).reshape([-1 if axis == dim else 1 for axis in range(len(dims))])
    return factor_of


def bell_draw(own_key, dims, scale, limit, cuts=(), dtype=jnp.bfloat16):
    drawn = jax.random.normal(own_key, dims, jnp.float32) * scale
    if len(cuts) > 0:
        drawn = block_scale(own_key, dims, cuts, -0.22, 0.18) * drawn
    return jnp.clip(drawn, min=-limit, max=limit).astype(dtype)


def heavy_noise(own_key, dims, scale, most, pieces, heavy, kind=jnp.bfloat16):
    entries = scale * jax.random.normal(own_key, dims, jnp.float32)
    if pieces:
        entries = entries * block_scale(own_key, dims, pieces, -0.22, 0.18)
    return jnp.clip(spiked(entries, jax.random.fold_in(own_key, 3), *heavy), -most, most).astype(kind)


def setup_inputs(seed: int = 0, part: int = 0) -> dict:
    streams_of = jax.random.split(jax.random.key(seed), 5)
    part_splits = jax.random.split(jax.random.fold_in(streams_of[4], part), 5)
    return {
        "tokens_q": bell_draw(part_splits[0], (STEPS, TOK, D), 1.0, 6.0, ((2, 16),)),
        "token_scale": jnp.clip(jnp.exp(jax.random.uniform(part_splits[1], (STEPS, TOK), jnp.float32, math.log(0.5), math.log(4.0))), 0.5, 4.0),
        "weight_in": bell_draw(streams_of[2], (D, FF), D ** -0.5, 0.0625, ((0, 2), (1, 8))),
        "weight_out": heavy_noise(streams_of[3], (FF, D), FF ** -0.5, 0.046875, ((0, 8), (1, 2)), (0, 1, 8, 2.0)),
    }


def reference(tokens_q, token_scale, weight_in, weight_out):
    quant_list = []
    scale_list = []
    for step_index in range(STEPS):
        pre = token_scale[step_index][:, None] * jnp.dot(tokens_q[step_index], weight_in, preferred_element_type=jnp.float32)
        hidden = jax.nn.gelu(pre, approximate=False).astype(jnp.bfloat16)
        full_out = jnp.dot(hidden, weight_out, preferred_element_type=jnp.float32)
        peak = jnp.max(jnp.abs(full_out), axis=1) + 1e-6
        quant_list.append((full_out / peak[:, None]).astype(jnp.bfloat16))
        scale_list.append(peak)
    return jnp.stack(quant_list), jnp.stack(scale_list)
```

```python
import functools

import jax
import jax.numpy as jnp
from jax import lax
from jax.experimental import pallas as pl
from jax.experimental.pallas import tpu as pltpu
from jax.sharding import PartitionSpec as P

F32, BF16 = jnp.float32, jnp.bfloat16


def divisor(size, most):
    best = 128
    for tile in range(128, most + 1, 128):
        if size % tile == 0:
            best = tile
    return best


def cost(rows, depth, columns, extra=0):
    return pl.CostEstimate(
        flops=2 * rows * depth * columns,
        bytes_accessed=2 * depth * columns + extra,
        transcendentals=0,
    )


def gather_matmul_kernel(block, tile, with_total, *refs):
    meta, tokens, weight = refs[:3]
    total = refs[3] if with_total else None
    out, held, sems = refs[-3:]
    step, steps = pl.program_id(0), pl.num_programs(0)
    pieces = tokens.shape[1] // block

    def copy(at, slot, piece):
        return pltpu.make_async_copy(
            weight.at[
                pl.ds(pl.multiple_of(meta[1 + piece] * block, 16), block),
                pl.ds(pl.multiple_of(meta[0] + at * tile, 128), tile),
            ],
            held.at[slot, pl.ds(piece * block, block)],
            sems.at[slot, piece],
        )

    @pl.when(step == 0)
    def _():
        for piece in range(pieces):
            copy(step, 0, piece).start()

    @pl.when(step + 1 < steps)
    def _():
        for piece in range(pieces):
            copy(step + 1, (step + 1) % 2, piece).start()

    slot = step % 2
    for piece in range(pieces):
        copy(step, slot, piece).wait()
    result = jnp.dot(tokens[...], held[slot], preferred_element_type=F32)
    if with_total:
        result = result + total[...]
    out[...] = result.astype(out.dtype)


def gather_matmul(meta, tokens, weight, total, columns, tile, block, total_column=None):
    rows, depth = tokens.shape
    pieces = depth // block
    in_specs = [
        pl.BlockSpec((rows, depth), lambda j, meta: (0, 0)),
        pl.BlockSpec(memory_space=pl.ANY),
    ]
    operands = [tokens, weight]
    if total is not None:
        in_specs.append(pl.BlockSpec((rows, tile), lambda j, meta: (0, meta[0] // tile + j)))
        operands.append(total)
    return pl.pallas_call(
        functools.partial(gather_matmul_kernel, block, tile, total is not None),
        grid_spec=pltpu.PrefetchScalarGridSpec(
            num_scalar_prefetch=1,
            grid=(columns // tile,),
            in_specs=in_specs,
            out_specs=pl.BlockSpec((rows, tile), lambda j, meta: (0, j)),
            scratch_shapes=[
                pltpu.VMEM((2, depth, tile), BF16),
                pltpu.SemaphoreType.DMA((2, pieces)),
            ],
        ),
        out_shape=jax.ShapeDtypeStruct((rows, columns), F32),
        compiler_params=pltpu.CompilerParams(vmem_limit_bytes=32 << 20),
        cost_estimate=cost(rows, depth, columns, 8 * rows * columns),
    )(meta, *operands)


def block_matmul_kernel(width, window, depth_tile, half_steps, blocks, *refs):
    meta, mine, other, weight = refs[:4]
    outs = refs[4 : 4 + blocks]
    held, total, sems = refs[4 + blocks :]
    step, steps = pl.program_id(0), pl.num_programs(0)
    core, half = meta[0], half_steps * depth_tile

    def copy(at, slot, block):
        side = jnp.where(at < half_steps, core, 1 - core)
        row = side * half + (at % half_steps) * depth_tile
        return pltpu.make_async_copy(
            weight.at[
                pl.ds(pl.multiple_of(row, 128), depth_tile),
                pl.ds(pl.multiple_of(meta[1 + 2 * block] * 128, 128), window),
            ],
            held.at[slot, :, pl.ds(block * window, window)],
            sems.at[slot, block],
        )

    @pl.when(step == 0)
    def _():
        for block in range(blocks):
            copy(step, 0, block).start()

    @pl.when(step + 1 < steps)
    def _():
        for block in range(blocks):
            copy(step + 1, (step + 1) % 2, block).start()

    slot = step % 2
    for block in range(blocks):
        copy(step, slot, block).wait()

    @pl.when(step == 0)
    def _():
        total[...] = jnp.dot(mine[...], held[slot], preferred_element_type=F32)

    @pl.when((step > 0) & (step < half_steps))
    def _():
        total[...] += jnp.dot(mine[...], held[slot], preferred_element_type=F32)

    @pl.when(step >= half_steps)
    def _():
        total[...] += jnp.dot(other[...], held[slot], preferred_element_type=F32)

    @pl.when(step + 1 == steps)
    def _():
        for block in range(blocks):
            value = total[:, block * window : (block + 1) * window]
            shifted = pltpu.roll(value, window - (window - width), 1) if window > width else value
            value = jnp.where(meta[2 + 2 * block] == 1, shifted, value)
            outs[block][...] = value[:, :width].astype(outs[block].dtype)


def block_matmul(core, shards, mine, other, weight, width, dtype):
    rows, half = mine.shape
    window = -(-width // 128) * 128
    depth_tile = divisor(half, 1152)
    half_steps = half // depth_tile
    blocks = len(shards)
    meta = [core]
    for shard in shards:
        meta += [shard * width // 128, (shard * width % 128 > 0).astype(jnp.int32)]
    meta = jnp.stack(meta).astype(jnp.int32)
    return pl.pallas_call(
        functools.partial(block_matmul_kernel, width, window, depth_tile, half_steps, blocks),
        grid_spec=pltpu.PrefetchScalarGridSpec(
            num_scalar_prefetch=1,
            grid=(2 * half_steps,),
            in_specs=[
                pl.BlockSpec((rows, depth_tile), lambda k, meta: (0, jnp.minimum(k, half_steps - 1))),
                pl.BlockSpec((rows, depth_tile), lambda k, meta: (0, jnp.maximum(k - half_steps, 0))),
                pl.BlockSpec(memory_space=pl.ANY),
            ],
            out_specs=[pl.BlockSpec((rows, width), lambda k, meta: (0, 0))] * blocks,
            scratch_shapes=[
                pltpu.VMEM((2, depth_tile, blocks * window), BF16),
                pltpu.VMEM((rows, blocks * window), F32),
                pltpu.SemaphoreType.DMA((2, blocks)),
            ],
        ),
        out_shape=[jax.ShapeDtypeStruct((rows, width), dtype)] * blocks,
        compiler_params=pltpu.CompilerParams(vmem_limit_bytes=32 << 20),
        cost_estimate=cost(rows, 2 * half, blocks * window, 4 * rows * half),
    )(meta, mine, other, weight)


def gelu(pre):
    return (0.5 * pre * (1.0 + lax.erf(pre * 0.7071067811865476))).astype(BF16)


def peak_over(value, n):
    value = jnp.maximum(value, lax.ppermute(value, "mdl", [(0, 1), (1, 0)]))
    reach = 1
    while reach < n:
        value = jnp.maximum(value, lax.ppermute(value, "hid", [(i, i ^ reach) for i in range(n)]))
        reach *= 2
    return value


def ring_layer(tokens_q, token_scale, weight_in, weight_out):
    n = lax.axis_size("hid")
    steps, step_rows, width = tokens_q.shape
    rows = steps * step_rows
    cut = rows // 2
    hidden_width = weight_in.shape[1]
    half = hidden_width // 2
    core = lax.axis_index("mdl")
    me = lax.axis_index("hid")
    order = [2 * i for i in range(n // 2)] + [2 * i + 1 for i in reversed(range(n // 2))]
    rightward = [(order[i], order[(i + 1) % n]) for i in range(n)]
    leftward = [(b, a) for a, b in rightward]
    place = jnp.where(me % 2 == 0, me // 2, n - 1 - me // 2)

    def at(offset):
        p = (place + offset + n) % n
        return jnp.where(p < n // 2, 2 * p, 2 * (n - 1 - p) + 1)

    def right(value):
        return lax.ppermute(value, "hid", rightward)

    def left(value):
        return lax.ppermute(value, "hid", leftward)

    def meta(column, offsets):
        return jnp.stack([jnp.asarray(column, jnp.int32)] + [at(k) for k in offsets]).astype(jnp.int32)

    own = tokens_q.reshape(rows, width)
    reach = n // 2
    going_right, going_left = own, own
    tile = divisor(hidden_width, 1152)
    total, waiting, offsets = None, [own], [0]
    for hop in range(1, reach):
        going_right, going_left = right(going_right), left(going_left)
        waiting += [going_right, going_left]
        offsets += [-hop, hop]
        total = gather_matmul(
            meta(0, offsets), jnp.concatenate(waiting, 1), weight_in, total, hidden_width, tile, width
        )
        waiting, offsets = [], []
    last = jnp.concatenate([right(going_right[:cut]), left(going_left[cut:])], 0)

    scale = token_scale.reshape(rows, 1)
    half_tile = divisor(half, 768)
    away = gather_matmul(meta((1 - core) * half, [reach]), last, weight_in, total, half, half_tile, width)
    received = lax.ppermute((away * scale).astype(BF16), "mdl", [(0, 1), (1, 0)])
    kept = gather_matmul(meta(core * half, [reach]), last, weight_in, total, half, half_tile, width)
    mine = gelu(kept * scale + received.astype(F32))
    other = lax.ppermute(mine, "mdl", [(0, 1), (1, 0)])

    def partial(offsets, dtype=F32):
        return block_matmul(core, [at(k) for k in offsets], mine, other, weight_out, width, dtype)

    (far,) = partial([reach], BF16)
    from_left, from_right = right(far[:cut]), left(far[cut:])
    for hop in range(reach - 1, 0, -1):
        to_right, to_left = partial([hop, -hop])
        if hop == reach - 1:
            to_right = jnp.concatenate([to_right[:cut] + from_left.astype(F32), to_right[cut:]], 0)
            to_left = jnp.concatenate([to_left[:cut], to_left[cut:] + from_right.astype(F32)], 0)
        else:
            to_right = to_right + from_left.astype(F32)
            to_left = to_left + from_right.astype(F32)
        from_left, from_right = right(to_right.astype(BF16)), left(to_left.astype(BF16))
    (here,) = partial([0])
    full_out = here + from_left.astype(F32) + from_right.astype(F32)

    peak = peak_over(jnp.max(jnp.abs(full_out), axis=1).reshape(steps, step_rows), n) + 1e-6
    quantized = (full_out.reshape(steps, step_rows, width) / peak[:, :, None]).astype(BF16)
    return quantized, peak


def plain_layer(tokens_q, token_scale, weight_in, weight_out):
    steps, step_rows, width = tokens_q.shape
    rows = steps * step_rows
    tokens = lax.all_gather(tokens_q.reshape(rows, width), "hid", axis=1, tiled=True)
    partial_pre = jnp.dot(tokens, weight_in, preferred_element_type=F32) * token_scale.reshape(rows, 1)
    hidden = gelu(lax.psum(partial_pre, "mdl"))
    sums = lax.dot_general(weight_out, hidden, (((0,), (1,)), ((), ())), preferred_element_type=F32)
    columns = lax.psum_scatter(sums, "hid", scatter_dimension=0, tiled=True)
    full_out = columns.T.reshape(steps, step_rows, width)
    peak = lax.pmax(jnp.max(jnp.abs(full_out), axis=2), ("hid", "mdl")) + 1e-6
    return (full_out / peak[:, :, None]).astype(BF16), peak


def per_device(tokens_q, token_scale, weight_in, weight_out):
    n = lax.axis_size("hid")
    steps, step_rows, width = tokens_q.shape
    hidden_width = weight_in.shape[1]
    window = -(-width // 128) * 128
    ring = (
        n >= 4
        and n & (n - 1) == 0
        and lax.axis_size("mdl") == 2
        and width % 64 == 0
        and width > 128
        and window - width in (0, 64)
        and hidden_width % 256 == 0
        and weight_out.shape[1] == n * width
        and (steps * step_rows) % 32 == 0
    )
    layer = ring_layer if ring else plain_layer
    return layer(tokens_q, token_scale, weight_in, weight_out)


def solution(mesh):
    return jax.shard_map(
        per_device,
        mesh=mesh,
        in_specs=(
            P(None, "groups", ("mdl", "hid")),
            P(None, "groups"),
            P("mdl", "hid"),
            P("hid", "mdl"),
        ),
        out_specs=(P(None, "groups", ("mdl", "hid")), P(None, "groups")),
        check_vma=False,
    )
```

```python
import functools

import jax
import jax.numpy as jnp
from jax import lax
from jax.experimental import pallas as pl
from jax.experimental.pallas import tpu as pltpu
from jax.sharding import PartitionSpec as P

F32, BF16 = jnp.float32, jnp.bfloat16
ROWS = 256
SLOTS = 3


def divisor(size, most):
    best = 128
    for tile in range(128, most + 1, 128):
        if size % tile == 0:
            best = tile
    return best


def ring_order(n):
    return [2 * i for i in range(n // 2)] + [2 * i + 1 for i in reversed(range(n // 2))]


def ring_shard(n, offset):
    me = lax.axis_index("hid")
    place = jnp.where(lax.rem(me, 2) == 0, lax.div(me, 2), n - 1 - lax.div(me, 2))
    place = lax.rem(place + offset + n, n)
    return jnp.where(place < n // 2, 2 * place, 2 * (n - 1 - place) + 1)


def cost(rows, depth, columns, extra=0):
    return pl.CostEstimate(
        flops=2 * rows * depth * columns,
        bytes_accessed=2 * depth * columns + extra,
        transcendentals=0,
    )


def gather_matmul_kernel(n, offsets, block, tile, counts, with_total, split, *refs):
    pieces = len(counts)
    tokens, refs = refs[: sum(counts)], refs[sum(counts) :]
    weight, refs = refs[0], refs[1:]
    total, refs = (refs[0], refs[1:]) if with_total else (None, refs)
    scale, refs = (refs[0], refs[1:]) if split else (None, refs)
    outs, (stacked, turned, held, sems) = refs[:-4], refs[-4:]
    depth, columns = pieces * block, weight.shape[1]
    tiles = columns // tile
    shards = [ring_shard(n, offset) for offset in offsets]
    first = (1 - lax.axis_index("mdl")) * (columns // 2)

    def copies(at):
        return [
            pltpu.make_async_copy(
                weight.at[
                    pl.ds(pl.multiple_of(shards[piece] * block, 16), block),
                    pl.ds(pl.multiple_of(lax.rem(first + at * tile, columns), 128), tile),
                ],
                held.at[at % SLOTS, pl.ds(piece * block, block)],
                sems.at[at % SLOTS, piece],
            )
            for piece in range(pieces)
        ]

    for at in range(min(SLOTS - 1, tiles)):
        for one in copies(at):
            one.start()
    index = 0
    for piece, count in enumerate(counts):
        lane = 0
        for ref in tokens[index : index + count]:
            stacked[piece * block : (piece + 1) * block, lane : lane + ref.shape[1]] = ref[...]
            lane += ref.shape[1]
        index += count
    if stacked.shape[0] > depth:
        stacked[depth:, :] = jnp.zeros((stacked.shape[0] - depth, stacked.shape[1]), BF16)
    turned[...] = stacked[...].T
    for at in range(tiles):
        if at + SLOTS - 1 < tiles:
            for one in copies(at + SLOTS - 1):
                one.start()
        for one in copies(at):
            one.wait()
        for top in range(0, turned.shape[0], ROWS):
            rows = slice(top, min(top + ROWS, turned.shape[0]))
            result = jnp.dot(turned[rows, :depth], held[at % SLOTS], preferred_element_type=F32)
            if with_total:
                result = result + total[rows, at * tile : (at + 1) * tile]
            if split:
                result = result * scale[rows]
            out = outs[at * len(outs) // tiles]
            low = at % (tiles // len(outs)) * tile
            out[rows, low : low + tile] = result.astype(out.dtype)


def gather_matmul(n, offsets, chunks, weight, total=None, scale=None):
    counts = tuple(len(chunk) for chunk in chunks)
    flat = [part for chunk in chunks for part in chunk]
    block, columns = flat[0].shape[0], weight.shape[1]
    rows = sum(part.shape[1] for part in chunks[0])
    depth = block * len(chunks)
    padded = -(-depth // 128) * 128
    tile = divisor(columns // 2, 768)
    vmem = pl.BlockSpec(memory_space=pltpu.VMEM)
    split = scale is not None
    operands = flat + [weight] + [extra for extra in (total, scale) if extra is not None]
    in_specs = [vmem] * len(operands)
    in_specs[len(flat)] = pl.BlockSpec(memory_space=pl.ANY)
    halves = [jax.ShapeDtypeStruct((rows, columns // 2), dtype) for dtype in (BF16, F32)]
    return pl.pallas_call(
        functools.partial(gather_matmul_kernel, n, tuple(offsets), block, tile, counts, total is not None, split),
        in_specs=in_specs,
        out_specs=[vmem, vmem] if split else vmem,
        scratch_shapes=[
            pltpu.VMEM((padded, rows), BF16),
            pltpu.VMEM((rows, padded), BF16),
            pltpu.VMEM((SLOTS, depth, tile), BF16),
            pltpu.SemaphoreType.DMA((SLOTS, len(chunks))),
        ],
        out_shape=halves if split else jax.ShapeDtypeStruct((rows, columns), F32),
        input_output_aliases={1 + len(flat): 0} if total is not None and not split else {},
        compiler_params=pltpu.CompilerParams(vmem_limit_bytes=14 << 20),
        cost_estimate=cost(rows, depth, columns),
    )(*operands)


def block_matmul_kernel(n, offsets, width, window, depth, sides, with_start, *refs):
    blocks = len(offsets)
    hidden, refs = refs[: len(sides)], refs[len(sides) :]
    weight, refs = refs[0], refs[1:]
    starts, refs = (refs[:blocks], refs[blocks:]) if with_start else (None, refs)
    outs, refs = refs[:blocks], refs[blocks:]
    held, total, turned, sems = refs
    core, (rows, half) = lax.axis_index("mdl"), hidden[0].shape
    columns = [ring_shard(n, offset) * width for offset in offsets]
    pieces = [(0, 0, depth), (0, depth, half)] + [(index, 0, half) for index in range(1, len(sides))]

    def copies(number):
        index, low, high = pieces[number]
        row = jnp.where(sides[index] == 0, core, 1 - core) * half + low
        return [
            pltpu.make_async_copy(
                weight.at[
                    pl.ds(pl.multiple_of(row, 128), high - low),
                    pl.ds(pl.multiple_of(lax.div(columns[block], 128) * 128, 128), window),
                ],
                held.at[pl.ds(index * half + low, high - low), pl.ds(block * window, window)],
                sems.at[number, block],
            )
            for block in range(blocks)
        ]

    for number in range(len(pieces)):
        for one in copies(number):
            one.start()
    for number, (index, low, high) in enumerate(pieces):
        for one in copies(number):
            one.wait()
        for top in range(0, rows, ROWS):
            here = slice(top, min(top + ROWS, rows))
            part = jnp.dot(
                hidden[index][here, low:high],
                held[index * half + low : index * half + high],
                preferred_element_type=F32,
            )
            if number > 0:
                part = total[here] + part
            if number + 1 < len(pieces):
                total[here] = part
            else:
                turned[:, here] = part.T
    for block in range(blocks):
        low = pl.multiple_of(block * window + lax.rem(columns[block], 128), 8)
        value = turned[pl.ds(low, width), :]
        if with_start:
            value = value + starts[block][...]
        outs[block][...] = value.astype(outs[block].dtype)


def block_matmul(n, offsets, sides, hidden, weight, width, starts=None, dtype=F32):
    rows, half = hidden[0].shape
    window = -(-width // 128) * 128
    blocks, both = len(offsets), len(sides) * half
    depth = divisor(half, 768)
    vmem = pl.BlockSpec(memory_space=pltpu.VMEM)
    starts = [] if starts is None else starts
    return pl.pallas_call(
        functools.partial(block_matmul_kernel, n, tuple(offsets), width, window, depth, sides, bool(starts)),
        in_specs=[vmem] * len(sides) + [pl.BlockSpec(memory_space=pl.ANY)] + [vmem] * len(starts),
        out_specs=[vmem] * blocks,
        scratch_shapes=[
            pltpu.VMEM((both, blocks * window), BF16),
            pltpu.VMEM((rows, blocks * window), F32),
            pltpu.VMEM((blocks * window, rows), F32),
            pltpu.SemaphoreType.DMA((1 + len(sides), blocks)),
        ],
        out_shape=[jax.ShapeDtypeStruct((width, rows), dtype)] * blocks,
        compiler_params=pltpu.CompilerParams(vmem_limit_bytes=22 << 20),
        cost_estimate=cost(rows, both, blocks * window),
    )(*hidden, weight, *starts)


def gelu(pre):
    return (0.5 * pre * (1.0 + lax.erf(pre * 0.7071067811865476))).astype(BF16)


def peak_over(value, n):
    value = jnp.maximum(value, lax.ppermute(value, "mdl", [(0, 1), (1, 0)]))
    reach = 1
    while reach < n:
        value = jnp.maximum(value, lax.ppermute(value, "hid", [(i, i ^ reach) for i in range(n)]))
        reach *= 2
    return value


def ring_layer(tokens_q, token_scale, weight_in, weight_out):
    n = lax.axis_size("hid")
    steps, step_rows, width = tokens_q.shape
    rows = steps * step_rows
    cut = rows // 2
    order = ring_order(n)
    rightward = [(order[i], order[(i + 1) % n]) for i in range(n)]
    leftward = [(b, a) for a, b in rightward]

    def right(value):
        return lax.ppermute(value, "hid", rightward)

    def left(value):
        return lax.ppermute(value, "hid", leftward)

    own = tokens_q.reshape(rows, width).T
    reach = n // 2
    scale = token_scale.reshape(rows, 1)

    def multiply(offsets, chunks, total, **kind):
        return gather_matmul(n, offsets, chunks, weight_in, total, **kind)

    going_right, going_left = right(own), left(own)
    total = multiply([0], [[own]], None)
    for hop in range(1, reach):
        going_right, going_left, total = lax.optimization_barrier((going_right, going_left, total))
        chunks, offsets = [[going_right], [going_left]], [-hop, hop]
        if hop < reach - 1:
            going_right, going_left = right(going_right), left(going_left)
        else:
            last = [right(going_right[:, :cut]), left(going_left[:, cut:])]
        total = multiply(offsets, chunks, total)
    *last, total = lax.optimization_barrier((*last, total))

    away, kept = multiply([reach], [last], total, scale=scale)
    received = lax.ppermute(away, "mdl", [(0, 1), (1, 0)])
    mine = gelu(kept + received.astype(F32))
    other = lax.ppermute(mine, "mdl", [(0, 1), (1, 0)])

    def partial(offsets, sides=(0, 1), **kind):
        hidden = [(mine, other)[side] for side in sides]
        return block_matmul(n, offsets, sides, hidden, weight_out, width, **kind)

    begun = partial([reach], sides=(0,))
    (far,) = partial([reach], sides=(1,), starts=begun, dtype=BF16)
    from_left, from_right = right(far[:, :cut]), left(far[:, cut:])
    for hop in range(reach - 1, 0, -1):
        to_right, to_left = partial([hop, -hop])
        from_left, from_right, to_right, to_left = lax.optimization_barrier((from_left, from_right, to_right, to_left))
        if hop == reach - 1:
            to_right = jnp.concatenate([to_right[:, :cut] + from_left.astype(F32), to_right[:, cut:]], 1)
            to_left = jnp.concatenate([to_left[:, :cut], to_left[:, cut:] + from_right.astype(F32)], 1)
        else:
            to_right = to_right + from_left.astype(F32)
            to_left = to_left + from_right.astype(F32)
        to_right, to_left = lax.optimization_barrier((to_right.astype(BF16), to_left.astype(BF16)))
        from_left, from_right = right(to_right), left(to_left)
    (here,) = partial([0])
    from_left, from_right, here = lax.optimization_barrier((from_left, from_right, here))
    full_out = here + from_left.astype(F32) + from_right.astype(F32)

    peak = peak_over(jnp.max(jnp.abs(full_out), axis=0).reshape(steps, step_rows), n) + 1e-6
    quantized = (full_out / peak.reshape(1, rows)).astype(BF16)
    return quantized.T.reshape(steps, step_rows, width), peak


def plain_layer(tokens_q, token_scale, weight_in, weight_out):
    steps, step_rows, width = tokens_q.shape
    rows = steps * step_rows
    tokens = lax.all_gather(tokens_q.reshape(rows, width), "hid", axis=1, tiled=True)
    partial_pre = jnp.dot(tokens, weight_in, preferred_element_type=F32) * token_scale.reshape(rows, 1)
    hidden = gelu(lax.psum(partial_pre, "mdl"))
    sums = lax.dot_general(weight_out, hidden, (((0,), (1,)), ((), ())), preferred_element_type=F32)
    columns = lax.psum_scatter(sums, "hid", scatter_dimension=0, tiled=True)
    full_out = columns.T.reshape(steps, step_rows, width)
    peak = lax.pmax(jnp.max(jnp.abs(full_out), axis=2), ("hid", "mdl")) + 1e-6
    return (full_out / peak[:, :, None]).astype(BF16), peak


def per_device(tokens_q, token_scale, weight_in, weight_out):
    n = lax.axis_size("hid")
    steps, step_rows, width = tokens_q.shape
    hidden_width = weight_in.shape[1]
    window = -(-width // 128) * 128
    ring = (
        n >= 4
        and n & (n - 1) == 0
        and lax.axis_size("mdl") == 2
        and width % 64 == 0
        and width > 128
        and window - width in (0, 64)
        and hidden_width % 256 == 0
        and weight_out.shape[1] == n * width
        and (steps * step_rows) % 32 == 0
    )
    layer = ring_layer if ring else plain_layer
    return layer(tokens_q, token_scale, weight_in, weight_out)


def solution(mesh):
    return jax.shard_map(
        per_device,
        mesh=mesh,
        in_specs=(
            P(None, "groups", ("mdl", "hid")),
            P(None, "groups"),
            P("mdl", "hid"),
            P("hid", "mdl"),
        ),
        out_specs=(P(None, "groups", ("mdl", "hid")), P(None, "groups")),
        check_vma=False,
    )
```

```python
import functools

import jax
import jax.numpy as jnp
from jax import lax
from jax.experimental import pallas as pl
from jax.experimental.pallas import tpu as pltpu
from jax.sharding import PartitionSpec as P

F32, BF16 = jnp.float32, jnp.bfloat16
ROWS = 256
SLOTS = 3


def divisor(size, most):
    best = 128
    for tile in range(128, most + 1, 128):
        if size % tile == 0:
            best = tile
    return best


def ring_order(n):
    return [2 * i for i in range(n // 2)] + [2 * i + 1 for i in reversed(range(n // 2))]


def ring_shard(n, offset):
    me = lax.axis_index("hid")
    place = jnp.where(lax.rem(me, 2) == 0, lax.div(me, 2), n - 1 - lax.div(me, 2))
    place = lax.rem(place + offset + n, n)
    return jnp.where(place < n // 2, 2 * place, 2 * (n - 1 - place) + 1)


def cost(rows, depth, columns, extra=0):
    return pl.CostEstimate(
        flops=2 * rows * depth * columns,
        bytes_accessed=2 * depth * columns + extra,
        transcendentals=0,
    )


def gather_matmul_kernel(n, offsets, block, tile, span, counts, with_total, with_scale, in_place, *refs):
    pieces = len(counts)
    tokens, refs = refs[: sum(counts)], refs[sum(counts) :]
    weight, refs = refs[0], refs[1:]
    total, refs = (refs[0], refs[1:]) if with_total else (None, refs)
    scale, refs = (refs[0], refs[1:]) if with_scale else (None, refs)
    factors, refs = (refs[-1], refs[:-1]) if with_scale else (None, refs)
    out, stacked, turned, held, sems = refs
    depth, columns = pieces * block, weight.shape[1]
    shards = [ring_shard(n, offset) for offset in offsets]
    first = (1 - lax.axis_index("mdl")) * (columns // 2)

    def copies(at):
        return [
            pltpu.make_async_copy(
                weight.at[
                    pl.ds(pl.multiple_of(shards[piece] * block, 16), block),
                    pl.ds(pl.multiple_of(lax.rem(first + at * tile, columns), 128), tile),
                ],
                held.at[at % SLOTS, pl.ds(piece * block, block)],
                sems.at[at % SLOTS, piece],
            )
            for piece in range(pieces)
        ]

    for at in range(span[0], min(span[0] + SLOTS - 1, span[1])):
        for one in copies(at):
            one.start()
    index = 0
    for piece, count in enumerate(counts):
        lane = 0
        for ref in tokens[index : index + count]:
            stacked[piece * block : (piece + 1) * block, lane : lane + ref.shape[1]] = ref[...]
            lane += ref.shape[1]
        index += count
    if stacked.shape[0] > depth:
        stacked[depth:, :] = jnp.zeros((stacked.shape[0] - depth, stacked.shape[1]), BF16)
    turned[...] = stacked[...].T
    if with_scale:
        for index in range(factors.shape[0]):
            factors[index] = jnp.broadcast_to(scale[index : index + 1, :], (128, scale.shape[1])).T
    for at in range(*span):
        if at + SLOTS - 1 < span[1]:
            for one in copies(at + SLOTS - 1):
                one.start()
        for one in copies(at):
            one.wait()
        stride = turned.shape[0] // factors.shape[0] if with_scale else ROWS
        for top in range(0, turned.shape[0], stride):
            rows = slice(top, min(top + stride, turned.shape[0]))
            result = jnp.dot(turned[rows, :depth], held[at % SLOTS], preferred_element_type=F32)
            if with_total:
                result = result + total[rows, at * tile : (at + 1) * tile]
            if with_scale:
                result = result * factors[top // stride][:, :1]
            low = (at if in_place else at - span[0]) * tile
            out[rows, low : low + tile] = result.astype(out.dtype)


def gather_matmul(n, offsets, chunks, weight, total=None, half=None, scale=None, dtype=F32):
    counts = tuple(len(chunk) for chunk in chunks)
    flat = [part for chunk in chunks for part in chunk]
    block, columns = flat[0].shape[0], weight.shape[1]
    rows = sum(part.shape[1] for part in chunks[0])
    depth = block * len(chunks)
    padded = -(-depth // 128) * 128
    tile = divisor(columns // 2, 768)
    vmem = pl.BlockSpec(memory_space=pltpu.VMEM)
    whole = scale is None
    tiles = columns // tile
    span = {None: (0, tiles), 0: (0, tiles // 2), 1: (tiles // 2, tiles)}[half]
    operands = flat + [weight] + [extra for extra in (total, scale) if extra is not None]
    in_specs = [vmem] * len(operands)
    in_specs[len(flat)] = pl.BlockSpec(memory_space=pl.ANY)
    return pl.pallas_call(
        functools.partial(
            gather_matmul_kernel, n, tuple(offsets), block, tile, span, counts, total is not None, not whole, whole
        ),
        in_specs=in_specs,
        out_specs=vmem,
        scratch_shapes=[
            pltpu.VMEM((padded, rows), BF16),
            pltpu.VMEM((rows, padded), BF16),
            pltpu.VMEM((SLOTS, depth, tile), BF16),
            pltpu.SemaphoreType.DMA((SLOTS, len(chunks))),
        ]
        + ([] if whole else [pltpu.VMEM((scale.shape[0], scale.shape[1], 128), F32)]),
        out_shape=jax.ShapeDtypeStruct((rows, (span[1] - span[0]) * tile if not whole else columns), dtype),
        input_output_aliases={1 + len(flat): 0} if total is not None and whole else {},
        compiler_params=pltpu.CompilerParams(vmem_limit_bytes=14 << 20),
        cost_estimate=cost(rows, depth, (span[1] - span[0]) * tile),
    )(*operands)


def block_matmul_kernel(n, offsets, width, window, depth, sides, with_start, *refs):
    blocks = len(offsets)
    hidden, refs = refs[: len(sides)], refs[len(sides) :]
    weight, refs = refs[0], refs[1:]
    starts, refs = (refs[:blocks], refs[blocks:]) if with_start else (None, refs)
    outs, refs = refs[:blocks], refs[blocks:]
    held, total, turned, sems = refs
    core, (rows, half) = lax.axis_index("mdl"), hidden[0].shape
    columns = [ring_shard(n, offset) * width for offset in offsets]
    pieces = [(0, 0, depth), (0, depth, half)] + [(index, 0, half) for index in range(1, len(sides))]

    def copies(number):
        index, low, high = pieces[number]
        row = jnp.where(sides[index] == 0, core, 1 - core) * half + low
        return [
            pltpu.make_async_copy(
                weight.at[
                    pl.ds(pl.multiple_of(row, 128), high - low),
                    pl.ds(pl.multiple_of(lax.div(columns[block], 128) * 128, 128), window),
                ],
                held.at[pl.ds(index * half + low, high - low), pl.ds(block * window, window)],
                sems.at[number, block],
            )
            for block in range(blocks)
        ]

    for number in range(len(pieces)):
        for one in copies(number):
            one.start()
    for number, (index, low, high) in enumerate(pieces):
        for one in copies(number):
            one.wait()
        for top in range(0, rows, ROWS):
            here = slice(top, min(top + ROWS, rows))
            part = jnp.dot(
                hidden[index][here, low:high],
                held[index * half + low : index * half + high],
                preferred_element_type=F32,
            )
            if number > 0:
                part = total[here] + part
            if number + 1 < len(pieces):
                total[here] = part
            else:
                turned[:, here] = part.T
    for block in range(blocks):
        low = pl.multiple_of(block * window + lax.rem(columns[block], 128), 8)
        value = turned[pl.ds(low, width), :]
        if with_start:
            value = value + starts[block][...]
        outs[block][...] = value.astype(outs[block].dtype)


def block_matmul(n, offsets, sides, hidden, weight, width, starts=None, dtype=F32):
    rows, half = hidden[0].shape
    window = -(-width // 128) * 128
    blocks, both = len(offsets), len(sides) * half
    depth = divisor(half, 768)
    vmem = pl.BlockSpec(memory_space=pltpu.VMEM)
    starts = [] if starts is None else starts
    return pl.pallas_call(
        functools.partial(block_matmul_kernel, n, tuple(offsets), width, window, depth, sides, bool(starts)),
        in_specs=[vmem] * len(sides) + [pl.BlockSpec(memory_space=pl.ANY)] + [vmem] * len(starts),
        out_specs=[vmem] * blocks,
        scratch_shapes=[
            pltpu.VMEM((both, blocks * window), BF16),
            pltpu.VMEM((rows, blocks * window), F32),
            pltpu.VMEM((blocks * window, rows), F32),
            pltpu.SemaphoreType.DMA((1 + len(sides), blocks)),
        ],
        out_shape=[jax.ShapeDtypeStruct((width, rows), dtype)] * blocks,
        compiler_params=pltpu.CompilerParams(vmem_limit_bytes=22 << 20),
        cost_estimate=cost(rows, both, blocks * window),
    )(*hidden, weight, *starts)


def gelu(pre):
    return (0.5 * pre * (1.0 + lax.erf(pre * 0.7071067811865476))).astype(BF16)


def peak_over(value, n):
    value = jnp.maximum(value, lax.ppermute(value, "mdl", [(0, 1), (1, 0)]))
    reach = 1
    while reach < n:
        value = jnp.maximum(value, lax.ppermute(value, "hid", [(i, i ^ reach) for i in range(n)]))
        reach *= 2
    return value


def ring_layer(tokens_q, token_scale, weight_in, weight_out):
    n = lax.axis_size("hid")
    steps, step_rows, width = tokens_q.shape
    rows = steps * step_rows
    cut = rows // 2
    order = ring_order(n)
    rightward = [(order[i], order[(i + 1) % n]) for i in range(n)]
    leftward = [(b, a) for a, b in rightward]

    def right(value):
        return lax.ppermute(value, "hid", rightward)

    def left(value):
        return lax.ppermute(value, "hid", leftward)

    own = tokens_q.reshape(rows, width).T
    reach = n // 2

    def multiply(offsets, chunks, total, **kind):
        return gather_matmul(n, offsets, chunks, weight_in, total, **kind)

    going_right, going_left = right(own), left(own)
    total = multiply([0], [[own]], None)
    for hop in range(1, reach):
        going_right, going_left, total = lax.optimization_barrier((going_right, going_left, total))
        chunks, offsets = [[going_right], [going_left]], [-hop, hop]
        if hop < reach - 1:
            going_right, going_left = right(going_right), left(going_left)
        else:
            last = [right(going_right[:, :cut]), left(going_left[:, cut:])]
        total = multiply(offsets, chunks, total, half=None if hop < reach - 1 else 0)
    *last, total = lax.optimization_barrier((*last, total))

    away = multiply([reach], [last], total, half=0, scale=token_scale, dtype=BF16)
    received = lax.ppermute(away, "mdl", [(0, 1), (1, 0)])
    kept = multiply([*offsets, reach], [*chunks, last], total, half=1, scale=token_scale)
    mine = gelu(kept + received.astype(F32))
    other = lax.ppermute(mine, "mdl", [(0, 1), (1, 0)])

    def partial(offsets, sides=(0, 1), **kind):
        hidden = [(mine, other)[side] for side in sides]
        return block_matmul(n, offsets, sides, hidden, weight_out, width, **kind)

    begun = partial([reach], sides=(0,))
    (far,) = partial([reach], sides=(1,), starts=begun, dtype=BF16)
    from_left, from_right = right(far[:, :cut]), left(far[:, cut:])
    for hop in range(reach - 1, 0, -1):
        to_right, to_left = partial([hop, -hop])
        from_left, from_right, to_right, to_left = lax.optimization_barrier((from_left, from_right, to_right, to_left))
        if hop == reach - 1:
            to_right = jnp.concatenate([to_right[:, :cut] + from_left.astype(F32), to_right[:, cut:]], 1)
            to_left = jnp.concatenate([to_left[:, :cut], to_left[:, cut:] + from_right.astype(F32)], 1)
        else:
            to_right = to_right + from_left.astype(F32)
            to_left = to_left + from_right.astype(F32)
        to_right, to_left = lax.optimization_barrier((to_right.astype(BF16), to_left.astype(BF16)))
        from_left, from_right = right(to_right), left(to_left)
    (here,) = partial([0])
    from_left, from_right, here = lax.optimization_barrier((from_left, from_right, here))
    full_out = here + from_left.astype(F32) + from_right.astype(F32)

    peak = peak_over(jnp.max(jnp.abs(full_out), axis=0).reshape(steps, step_rows), n) + 1e-6
    quantized = (full_out / peak.reshape(1, rows)).astype(BF16)
    return quantized.T.reshape(steps, step_rows, width), peak


def plain_layer(tokens_q, token_scale, weight_in, weight_out):
    steps, step_rows, width = tokens_q.shape
    rows = steps * step_rows
    tokens = lax.all_gather(tokens_q.reshape(rows, width), "hid", axis=1, tiled=True)
    partial_pre = jnp.dot(tokens, weight_in, preferred_element_type=F32) * token_scale.reshape(rows, 1)
    hidden = gelu(lax.psum(partial_pre, "mdl"))
    sums = lax.dot_general(weight_out, hidden, (((0,), (1,)), ((), ())), preferred_element_type=F32)
    columns = lax.psum_scatter(sums, "hid", scatter_dimension=0, tiled=True)
    full_out = columns.T.reshape(steps, step_rows, width)
    peak = lax.pmax(jnp.max(jnp.abs(full_out), axis=2), ("hid", "mdl")) + 1e-6
    return (full_out / peak[:, :, None]).astype(BF16), peak


def per_device(tokens_q, token_scale, weight_in, weight_out):
    n = lax.axis_size("hid")
    steps, step_rows, width = tokens_q.shape
    hidden_width = weight_in.shape[1]
    window = -(-width // 128) * 128
    ring = (
        n >= 4
        and n & (n - 1) == 0
        and lax.axis_size("mdl") == 2
        and width % 64 == 0
        and width > 128
        and window - width in (0, 64)
        and hidden_width % 256 == 0
        and weight_out.shape[1] == n * width
        and (steps * step_rows) % 32 == 0
    )
    layer = ring_layer if ring else plain_layer
    return layer(tokens_q, token_scale, weight_in, weight_out)


def solution(mesh):
    return jax.shard_map(
        per_device,
        mesh=mesh,
        in_specs=(
            P(None, "groups", ("mdl", "hid")),
            P(None, "groups"),
            P("mdl", "hid"),
            P("hid", "mdl"),
        ),
        out_specs=(P(None, "groups", ("mdl", "hid")), P(None, "groups")),
        check_vma=False,
    )
```

```python
import functools

import jax
import jax.numpy as jnp
from jax import lax
from jax.experimental import pallas as pl
from jax.experimental.pallas import tpu as pltpu
from jax.sharding import PartitionSpec as P

F32, BF16 = jnp.float32, jnp.bfloat16
ROWS = 256
SLOTS = 3


def divisor(size, most):
    best = 128
    for tile in range(128, most + 1, 128):
        if size % tile == 0:
            best = tile
    return best


def ring_order(n):
    return [2 * i for i in range(n // 2)] + [2 * i + 1 for i in reversed(range(n // 2))]


def ring_shard(n, offset):
    me = lax.axis_index("hid")
    place = jnp.where(lax.rem(me, 2) == 0, lax.div(me, 2), n - 1 - lax.div(me, 2))
    place = lax.rem(place + offset + n, n)
    return jnp.where(place < n // 2, 2 * place, 2 * (n - 1 - place) + 1)


def cost(rows, depth, columns, extra=0):
    return pl.CostEstimate(
        flops=2 * rows * depth * columns,
        bytes_accessed=2 * depth * columns + extra,
        transcendentals=0,
    )


def gather_matmul_kernel(n, offsets, block, tile, span, counts, with_total, with_scale, in_place, *refs):
    pieces = len(counts)
    tokens, refs = refs[: sum(counts)], refs[sum(counts) :]
    weight, refs = refs[0], refs[1:]
    total, refs = (refs[0], refs[1:]) if with_total else (None, refs)
    scale, refs = (refs[0], refs[1:]) if with_scale else (None, refs)
    factors, refs = (refs[-1], refs[:-1]) if with_scale else (None, refs)
    out, stacked, turned, held, sems = refs
    depth, columns = pieces * block, weight.shape[1]
    shards = [ring_shard(n, offset) for offset in offsets]
    first = (1 - lax.axis_index("mdl")) * (columns // 2)

    def copies(at):
        return [
            pltpu.make_async_copy(
                weight.at[
                    pl.ds(pl.multiple_of(shards[piece] * block, 16), block),
                    pl.ds(pl.multiple_of(lax.rem(first + at * tile, columns), 128), tile),
                ],
                held.at[at % SLOTS, pl.ds(piece * block, block)],
                sems.at[at % SLOTS, piece],
            )
            for piece in range(pieces)
        ]

    for at in range(span[0], min(span[0] + SLOTS - 1, span[1])):
        for one in copies(at):
            one.start()
    index = 0
    for piece, count in enumerate(counts):
        lane = 0
        for ref in tokens[index : index + count]:
            stacked[piece * block : (piece + 1) * block, lane : lane + ref.shape[1]] = ref[...]
            lane += ref.shape[1]
        index += count
    if stacked.shape[0] > depth:
        stacked[depth:, :] = jnp.zeros((stacked.shape[0] - depth, stacked.shape[1]), BF16)
    turned[...] = stacked[...].T
    if with_scale:
        for index in range(factors.shape[0]):
            factors[index] = jnp.broadcast_to(scale[index : index + 1, :], (128, scale.shape[1])).T
    for at in range(*span):
        if at + SLOTS - 1 < span[1]:
            for one in copies(at + SLOTS - 1):
                one.start()
        for one in copies(at):
            one.wait()
        stride = turned.shape[0] // factors.shape[0] if with_scale else ROWS
        for top in range(0, turned.shape[0], stride):
            rows = slice(top, min(top + stride, turned.shape[0]))
            result = jnp.dot(turned[rows, :depth], held[at % SLOTS], preferred_element_type=F32)
            if with_total:
                result = result + total[rows, at * tile : (at + 1) * tile]
            if with_scale:
                result = result * factors[top // stride][:, :1]
            low = (at if in_place else at - span[0]) * tile
            out[rows, low : low + tile] = result.astype(out.dtype)


def gather_matmul(n, offsets, chunks, weight, total=None, half=None, scale=None, dtype=F32):
    counts = tuple(len(chunk) for chunk in chunks)
    flat = [part for chunk in chunks for part in chunk]
    block, columns = flat[0].shape[0], weight.shape[1]
    rows = sum(part.shape[1] for part in chunks[0])
    depth = block * len(chunks)
    padded = -(-depth // 128) * 128
    tile = divisor(columns // 2, 768)
    vmem = pl.BlockSpec(memory_space=pltpu.VMEM)
    whole = scale is None
    tiles = columns // tile
    span = {None: (0, tiles), 0: (0, tiles // 2), 1: (tiles // 2, tiles)}[half]
    operands = flat + [weight] + [extra for extra in (total, scale) if extra is not None]
    in_specs = [vmem] * len(operands)
    in_specs[len(flat)] = pl.BlockSpec(memory_space=pl.ANY)
    return pl.pallas_call(
        functools.partial(
            gather_matmul_kernel, n, tuple(offsets), block, tile, span, counts, total is not None, not whole, whole
        ),
        in_specs=in_specs,
        out_specs=vmem,
        scratch_shapes=[
            pltpu.VMEM((padded, rows), BF16),
            pltpu.VMEM((rows, padded), BF16),
            pltpu.VMEM((SLOTS, depth, tile), BF16),
            pltpu.SemaphoreType.DMA((SLOTS, len(chunks))),
        ]
        + ([] if whole else [pltpu.VMEM((scale.shape[0], scale.shape[1], 128), F32)]),
        out_shape=jax.ShapeDtypeStruct((rows, (span[1] - span[0]) * tile if not whole else columns), dtype),
        input_output_aliases={1 + len(flat): 0} if total is not None and whole else {},
        compiler_params=pltpu.CompilerParams(vmem_limit_bytes=14 << 20),
        cost_estimate=cost(rows, depth, (span[1] - span[0]) * tile),
    )(*operands)


def block_matmul_kernel(n, offsets, width, window, depth, sides, with_start, *refs):
    blocks = len(offsets)
    hidden, refs = refs[: len(sides)], refs[len(sides) :]
    weight, refs = refs[0], refs[1:]
    starts, refs = (refs[:blocks], refs[blocks:]) if with_start else (None, refs)
    outs, refs = refs[:blocks], refs[blocks:]
    held, total, turned, sems = refs
    core, (rows, half) = lax.axis_index("mdl"), hidden[0].shape
    columns = [ring_shard(n, offset) * width for offset in offsets]
    pieces = [(0, 0, depth), (0, depth, half)] + [(index, 0, half) for index in range(1, len(sides))]

    def copies(number):
        index, low, high = pieces[number]
        row = jnp.where(sides[index] == 0, core, 1 - core) * half + low
        return [
            pltpu.make_async_copy(
                weight.at[
                    pl.ds(pl.multiple_of(row, 128), high - low),
                    pl.ds(pl.multiple_of(lax.div(columns[block], 128) * 128, 128), window),
                ],
                held.at[pl.ds(index * half + low, high - low), pl.ds(block * window, window)],
                sems.at[number, block],
            )
            for block in range(blocks)
        ]

    for number in range(len(pieces)):
        for one in copies(number):
            one.start()
    for number, (index, low, high) in enumerate(pieces):
        for one in copies(number):
            one.wait()
        for top in range(0, rows, ROWS):
            here = slice(top, min(top + ROWS, rows))
            part = jnp.dot(
                hidden[index][here, low:high],
                held[index * half + low : index * half + high],
                preferred_element_type=F32,
            )
            if number > 0:
                part = total[here] + part
            if number + 1 < len(pieces):
                total[here] = part
            else:
                turned[:, here] = part.T
    for block in range(blocks):
        low = pl.multiple_of(block * window + lax.rem(columns[block], 128), 8)
        value = turned[pl.ds(low, width), :]
        if with_start:
            value = value + starts[block][...]
        outs[block][...] = value.astype(outs[block].dtype)


def block_matmul(n, offsets, sides, hidden, weight, width, starts=None, dtype=F32):
    rows, half = hidden[0].shape
    window = -(-width // 128) * 128
    blocks, both = len(offsets), len(sides) * half
    depth = divisor(half, 768)
    vmem = pl.BlockSpec(memory_space=pltpu.VMEM)
    starts = [] if starts is None else starts
    return pl.pallas_call(
        functools.partial(block_matmul_kernel, n, tuple(offsets), width, window, depth, sides, bool(starts)),
        in_specs=[vmem] * len(sides) + [pl.BlockSpec(memory_space=pl.ANY)] + [vmem] * len(starts),
        out_specs=[vmem] * blocks,
        scratch_shapes=[
            pltpu.VMEM((both, blocks * window), BF16),
            pltpu.VMEM((rows, blocks * window), F32),
            pltpu.VMEM((blocks * window, rows), F32),
            pltpu.SemaphoreType.DMA((1 + len(sides), blocks)),
        ],
        out_shape=[jax.ShapeDtypeStruct((width, rows), dtype)] * blocks,
        compiler_params=pltpu.CompilerParams(vmem_limit_bytes=22 << 20),
        cost_estimate=cost(rows, both, blocks * window),
    )(*hidden, weight, *starts)


def gelu(pre):
    return (0.5 * pre * (1.0 + lax.erf(pre * 0.7071067811865476))).astype(BF16)


def peak_over(value, n):
    value = jnp.maximum(value, lax.ppermute(value, "mdl", [(0, 1), (1, 0)]))
    near = [lax.ppermute(value, "hid", [(i, i ^ flip) for i in range(n)]) for flip in (1, 2, 3)]
    value = functools.reduce(jnp.maximum, near, value)
    reach = 4
    while reach < n:
        value = jnp.maximum(value, lax.ppermute(value, "hid", [(i, i ^ reach) for i in range(n)]))
        reach *= 2
    return value


def ring_layer(tokens_q, token_scale, weight_in, weight_out):
    n = lax.axis_size("hid")
    steps, step_rows, width = tokens_q.shape
    rows = steps * step_rows
    cut = rows // 2
    order = ring_order(n)
    rightward = [(order[i], order[(i + 1) % n]) for i in range(n)]
    leftward = [(b, a) for a, b in rightward]

    def right(value):
        return lax.ppermute(value, "hid", rightward)

    def left(value):
        return lax.ppermute(value, "hid", leftward)

    own = tokens_q.reshape(rows, width).T
    reach = n // 2

    def multiply(offsets, chunks, total, **kind):
        return gather_matmul(n, offsets, chunks, weight_in, total, **kind)

    going_right, going_left = right(own), left(own)
    total = multiply([0], [[own]], None)
    for hop in range(1, reach):
        going_right, going_left, total = lax.optimization_barrier((going_right, going_left, total))
        chunks, offsets = [[going_right], [going_left]], [-hop, hop]
        if hop < reach - 1:
            going_right, going_left = right(going_right), left(going_left)
        else:
            last = [right(going_right[:, :cut]), left(going_left[:, cut:])]
        total = multiply(offsets, chunks, total, half=None if hop < reach - 1 else 0)
    *last, total = lax.optimization_barrier((*last, total))

    away = multiply([reach], [last], total, half=0, scale=token_scale, dtype=BF16)
    received = lax.ppermute(away, "mdl", [(0, 1), (1, 0)])
    kept = multiply([*offsets, reach], [*chunks, last], total, half=1, scale=token_scale)
    mine = gelu(kept + received.astype(F32))
    other = lax.ppermute(mine, "mdl", [(0, 1), (1, 0)])

    def partial(offsets, sides=(0, 1), **kind):
        hidden = [(mine, other)[side] for side in sides]
        return block_matmul(n, offsets, sides, hidden, weight_out, width, **kind)

    begun = partial([reach], sides=(0,))
    (far,) = partial([reach], sides=(1,), starts=begun, dtype=BF16)
    first = right(far[:, :cut]), left(far[:, cut:])
    second = None
    for hop in range(reach - 1, 0, -1):
        to_right, to_left = partial([hop, -hop])
        if second is None:
            go_right, go_left = to_right[:, cut:], to_left[:, :cut]
        else:
            *second, to_right, to_left = lax.optimization_barrier((*second, to_right, to_left))
            go_right, go_left = to_right[:, cut:] + second[0].astype(F32), to_left[:, :cut] + second[1].astype(F32)
        go_right, go_left = lax.optimization_barrier((go_right.astype(BF16), go_left.astype(BF16)))
        second = right(go_right), left(go_left)
        *first, to_right, to_left = lax.optimization_barrier((*first, to_right, to_left))
        go_right, go_left = to_right[:, :cut] + first[0].astype(F32), to_left[:, cut:] + first[1].astype(F32)
        go_right, go_left, mine, other = lax.optimization_barrier(
            (go_right.astype(BF16), go_left.astype(BF16), mine, other)
        )
        first = right(go_right), left(go_left)
    (here,) = partial([0])
    *first, here = lax.optimization_barrier((*first, here))
    full_out = here + jnp.concatenate(
        [
            first[0].astype(F32) + second[1].astype(F32),
            second[0].astype(F32) + first[1].astype(F32),
        ],
        1,
    )

    peak = peak_over(jnp.max(jnp.abs(full_out), axis=0).reshape(steps, step_rows), n) + 1e-6
    quantized = (full_out / peak.reshape(1, rows)).astype(BF16)
    return quantized.T.reshape(steps, step_rows, width), peak


def plain_layer(tokens_q, token_scale, weight_in, weight_out):
    steps, step_rows, width = tokens_q.shape
    rows = steps * step_rows
    tokens = lax.all_gather(tokens_q.reshape(rows, width), "hid", axis=1, tiled=True)
    partial_pre = jnp.dot(tokens, weight_in, preferred_element_type=F32) * token_scale.reshape(rows, 1)
    hidden = gelu(lax.psum(partial_pre, "mdl"))
    sums = lax.dot_general(weight_out, hidden, (((0,), (1,)), ((), ())), preferred_element_type=F32)
    columns = lax.psum_scatter(sums, "hid", scatter_dimension=0, tiled=True)
    full_out = columns.T.reshape(steps, step_rows, width)
    peak = lax.pmax(jnp.max(jnp.abs(full_out), axis=2), ("hid", "mdl")) + 1e-6
    return (full_out / peak[:, :, None]).astype(BF16), peak


def per_device(tokens_q, token_scale, weight_in, weight_out):
    n = lax.axis_size("hid")
    steps, step_rows, width = tokens_q.shape
    hidden_width = weight_in.shape[1]
    window = -(-width // 128) * 128
    ring = (
        n >= 4
        and n & (n - 1) == 0
        and lax.axis_size("mdl") == 2
        and width % 64 == 0
        and width > 128
        and window - width in (0, 64)
        and hidden_width % 256 == 0
        and weight_out.shape[1] == n * width
        and (steps * step_rows) % 32 == 0
    )
    layer = ring_layer if ring else plain_layer
    return layer(tokens_q, token_scale, weight_in, weight_out)


def solution(mesh):
    return jax.shard_map(
        per_device,
        mesh=mesh,
        in_specs=(
            P(None, "groups", ("mdl", "hid")),
            P(None, "groups"),
            P("mdl", "hid"),
            P("hid", "mdl"),
        ),
        out_specs=(P(None, "groups", ("mdl", "hid")), P(None, "groups")),
        check_vma=False,
    )
```

```python
import functools

import jax
import jax.numpy as jnp
from jax import lax
from jax.experimental import pallas as pl
from jax.experimental.pallas import tpu as pltpu
from jax.sharding import PartitionSpec as P

F32, BF16 = jnp.float32, jnp.bfloat16
ROWS = 256
SLOTS = 3


def divisor(size, most):
    best = 128
    for tile in range(128, most + 1, 128):
        if size % tile == 0:
            best = tile
    return best


def ring_order(n):
    return [2 * i for i in range(n // 2)] + [2 * i + 1 for i in reversed(range(n // 2))]


def ring_shard(n, offset):
    me = lax.axis_index("hid")
    place = jnp.where(lax.rem(me, 2) == 0, lax.div(me, 2), n - 1 - lax.div(me, 2))
    place = lax.rem(place + offset + n, n)
    return jnp.where(place < n // 2, 2 * place, 2 * (n - 1 - place) + 1)


def cost(rows, depth, columns, extra=0):
    return pl.CostEstimate(
        flops=2 * rows * depth * columns,
        bytes_accessed=2 * depth * columns + extra,
        transcendentals=0,
    )


def gather_matmul_kernel(n, offsets, block, cuts, counts, with_total, with_scale, in_place, *refs):
    pieces = len(counts)
    tokens, refs = refs[: sum(counts)], refs[sum(counts) :]
    weight, refs = refs[0], refs[1:]
    total, refs = (refs[0], refs[1:]) if with_total else (None, refs)
    scale, refs = (refs[0], refs[1:]) if with_scale else (None, refs)
    factors, refs = (refs[-1], refs[:-1]) if with_scale else (None, refs)
    out, stacked, turned, held, sems = refs
    depth, columns = pieces * block, weight.shape[1]
    shards = [ring_shard(n, offset) for offset in offsets]
    first = (1 - lax.axis_index("mdl")) * (columns // 2)

    def copies(at):
        low, size = cuts[at], cuts[at + 1] - cuts[at]
        return [
            pltpu.make_async_copy(
                weight.at[
                    pl.ds(pl.multiple_of(shards[piece] * block, 16), block),
                    pl.ds(pl.multiple_of(lax.rem(first + low, columns), 128), size),
                ],
                held.at[at % SLOTS, pl.ds(piece * block, block), pl.ds(0, size)],
                sems.at[at % SLOTS, piece],
            )
            for piece in range(pieces)
        ]

    for at in range(min(SLOTS, len(cuts)) - 1):
        for one in copies(at):
            one.start()
    index = 0
    for piece, count in enumerate(counts):
        lane = 0
        for ref in tokens[index : index + count]:
            stacked[piece * block : (piece + 1) * block, lane : lane + ref.shape[1]] = ref[...]
            lane += ref.shape[1]
        index += count
    if stacked.shape[0] > depth:
        stacked[depth:, :] = jnp.zeros((stacked.shape[0] - depth, stacked.shape[1]), BF16)
    turned[...] = stacked[...].T
    if with_scale:
        for index in range(factors.shape[0]):
            factors[index] = jnp.broadcast_to(scale[index : index + 1, :], (128, scale.shape[1])).T
    for at in range(len(cuts) - 1):
        if at + SLOTS < len(cuts):
            for one in copies(at + SLOTS - 1):
                one.start()
        for one in copies(at):
            one.wait()
        stride = turned.shape[0] // factors.shape[0] if with_scale else ROWS
        for top in range(0, turned.shape[0], stride):
            rows = slice(top, min(top + stride, turned.shape[0]))
            size = cuts[at + 1] - cuts[at]
            result = jnp.dot(turned[rows, :depth], held[at % SLOTS, :, :size], preferred_element_type=F32)
            if with_total:
                result = result + total[rows, cuts[at] : cuts[at + 1]]
            if with_scale:
                result = result * factors[top // stride][:, :1]
            low = cuts[at] if in_place else cuts[at] - cuts[0]
            out[rows, low : low + size] = result.astype(out.dtype)


def gather_matmul(n, offsets, chunks, weight, total=None, half=None, scale=None, dtype=F32):
    counts = tuple(len(chunk) for chunk in chunks)
    flat = [part for chunk in chunks for part in chunk]
    block, columns = flat[0].shape[0], weight.shape[1]
    rows = sum(part.shape[1] for part in chunks[0])
    depth = block * len(chunks)
    padded = -(-depth // 128) * 128
    tile = divisor(columns // 2, 768)
    vmem = pl.BlockSpec(memory_space=pltpu.VMEM)
    whole = scale is None
    low, high = {None: (0, columns), 0: (0, columns // 2), 1: (columns // 2, columns)}[half]
    cuts = tuple(range(low, high + 1, tile))
    if tile == 768:
        cuts = (low, low + 256, *cuts[1:])
    operands = flat + [weight] + [extra for extra in (total, scale) if extra is not None]
    in_specs = [vmem] * len(operands)
    in_specs[len(flat)] = pl.BlockSpec(memory_space=pl.ANY)
    return pl.pallas_call(
        functools.partial(
            gather_matmul_kernel, n, tuple(offsets), block, cuts, counts, total is not None, not whole, whole
        ),
        in_specs=in_specs,
        out_specs=vmem,
        scratch_shapes=[
            pltpu.VMEM((padded, rows), BF16),
            pltpu.VMEM((rows, padded), BF16),
            pltpu.VMEM((SLOTS, depth, tile), BF16),
            pltpu.SemaphoreType.DMA((SLOTS, len(chunks))),
        ]
        + ([] if whole else [pltpu.VMEM((scale.shape[0], scale.shape[1], 128), F32)]),
        out_shape=jax.ShapeDtypeStruct((rows, columns if whole else high - low), dtype),
        input_output_aliases={1 + len(flat): 0} if total is not None and whole else {},
        compiler_params=pltpu.CompilerParams(vmem_limit_bytes=14 << 20),
        cost_estimate=cost(rows, depth, high - low),
    )(*operands)


def block_matmul_kernel(n, offsets, width, window, depth, sides, with_start, *refs):
    blocks = len(offsets)
    hidden, refs = refs[: len(sides)], refs[len(sides) :]
    weight, refs = refs[0], refs[1:]
    starts, refs = (refs[:blocks], refs[blocks:]) if with_start else (None, refs)
    outs, refs = refs[:blocks], refs[blocks:]
    held, total, turned, sems = refs
    core, (rows, half) = lax.axis_index("mdl"), hidden[0].shape
    columns = [ring_shard(n, offset) * width for offset in offsets]
    pieces = [(0, 0, depth), (0, depth, half)] + [(index, 0, half) for index in range(1, len(sides))]

    def copies(number):
        index, low, high = pieces[number]
        row = jnp.where(sides[index] == 0, core, 1 - core) * half + low
        return [
            pltpu.make_async_copy(
                weight.at[
                    pl.ds(pl.multiple_of(row, 128), high - low),
                    pl.ds(pl.multiple_of(lax.div(columns[block], 128) * 128, 128), window),
                ],
                held.at[pl.ds(index * half + low, high - low), pl.ds(block * window, window)],
                sems.at[number, block],
            )
            for block in range(blocks)
        ]

    for number in range(len(pieces)):
        for one in copies(number):
            one.start()
    for number, (index, low, high) in enumerate(pieces):
        for one in copies(number):
            one.wait()
        for top in range(0, rows, ROWS):
            here = slice(top, min(top + ROWS, rows))
            part = jnp.dot(
                hidden[index][here, low:high],
                held[index * half + low : index * half + high],
                preferred_element_type=F32,
            )
            if number > 0:
                part = total[here] + part
            if number + 1 < len(pieces):
                total[here] = part
            else:
                turned[:, here] = part.T
    for block in range(blocks):
        low = pl.multiple_of(block * window + lax.rem(columns[block], 128), 8)
        value = turned[pl.ds(low, width), :]
        if with_start:
            value = value + starts[block][...]
        outs[block][...] = value.astype(outs[block].dtype)


def block_matmul(n, offsets, sides, hidden, weight, width, starts=None, dtype=F32):
    rows, half = hidden[0].shape
    window = -(-width // 128) * 128
    blocks, both = len(offsets), len(sides) * half
    depth = divisor(half, 768)
    vmem = pl.BlockSpec(memory_space=pltpu.VMEM)
    starts = [] if starts is None else starts
    return pl.pallas_call(
        functools.partial(block_matmul_kernel, n, tuple(offsets), width, window, depth, sides, bool(starts)),
        in_specs=[vmem] * len(sides) + [pl.BlockSpec(memory_space=pl.ANY)] + [vmem] * len(starts),
        out_specs=[vmem] * blocks,
        scratch_shapes=[
            pltpu.VMEM((both, blocks * window), BF16),
            pltpu.VMEM((rows, blocks * window), F32),
            pltpu.VMEM((blocks * window, rows), F32),
            pltpu.SemaphoreType.DMA((1 + len(sides), blocks)),
        ],
        out_shape=[jax.ShapeDtypeStruct((width, rows), dtype)] * blocks,
        compiler_params=pltpu.CompilerParams(vmem_limit_bytes=22 << 20),
        cost_estimate=cost(rows, both, blocks * window),
    )(*hidden, weight, *starts)


def gelu(pre):
    return (0.5 * pre * (1.0 + lax.erf(pre * 0.7071067811865476))).astype(BF16)


def peak_over(value, n):
    value = jnp.maximum(value, lax.ppermute(value, "mdl", [(0, 1), (1, 0)]))
    near = [lax.ppermute(value, "hid", [(i, i ^ flip) for i in range(n)]) for flip in (1, 2, 3)]
    value = functools.reduce(jnp.maximum, near, value)
    reach = 4
    while reach < n:
        value = jnp.maximum(value, lax.ppermute(value, "hid", [(i, i ^ reach) for i in range(n)]))
        reach *= 2
    return value


def ring_layer(tokens_q, token_scale, weight_in, weight_out):
    n = lax.axis_size("hid")
    steps, step_rows, width = tokens_q.shape
    rows = steps * step_rows
    cut = rows // 2
    order = ring_order(n)
    rightward = [(order[i], order[(i + 1) % n]) for i in range(n)]
    leftward = [(b, a) for a, b in rightward]

    def right(value):
        return lax.ppermute(value, "hid", rightward)

    def left(value):
        return lax.ppermute(value, "hid", leftward)

    own = tokens_q.reshape(rows, width).T
    reach = n // 2

    def multiply(offsets, chunks, total, **kind):
        return gather_matmul(n, offsets, chunks, weight_in, total, **kind)

    first = right(own[:, :cut]), left(own[:, cut:])
    second = right(own[:, cut:]), left(own[:, :cut])
    total = multiply([0], [[own]], None)
    for hop in range(1, reach):
        *first, total = lax.optimization_barrier((*first, total))
        ahead = right(first[0]), left(first[1])
        *second, total = lax.optimization_barrier((*second, total))
        chunks, offsets = [[first[0], second[0]], [second[1], first[1]]], [-hop, hop]
        total = multiply(offsets, chunks, total, half=None if hop < reach - 1 else 0)
        if hop < reach - 1:
            second = right(second[0]), left(second[1])
        first = ahead
    *last, total = lax.optimization_barrier((*first, total))

    away = multiply([reach], [last], total, half=0, scale=token_scale, dtype=BF16)
    received = lax.ppermute(away, "mdl", [(0, 1), (1, 0)])
    kept = multiply([*offsets, reach], [*chunks, last], total, half=1, scale=token_scale)
    mine = gelu(kept + received.astype(F32))
    other = lax.ppermute(mine, "mdl", [(0, 1), (1, 0)])

    def partial(offsets, sides=(0, 1), **kind):
        hidden = [(mine, other)[side] for side in sides]
        return block_matmul(n, offsets, sides, hidden, weight_out, width, **kind)

    begun = partial([reach], sides=(0,))
    (far,) = partial([reach], sides=(1,), starts=begun, dtype=BF16)
    first = right(far[:, :cut]), left(far[:, cut:])
    second = None
    for hop in range(reach - 1, 0, -1):
        to_right, to_left = partial([hop, -hop])
        if second is None:
            go_right, go_left = to_right[:, cut:], to_left[:, :cut]
        else:
            *second, to_right, to_left = lax.optimization_barrier((*second, to_right, to_left))
            go_right, go_left = to_right[:, cut:] + second[0].astype(F32), to_left[:, :cut] + second[1].astype(F32)
        go_right, go_left = lax.optimization_barrier((go_right.astype(BF16), go_left.astype(BF16)))
        second = right(go_right), left(go_left)
        *first, to_right, to_left = lax.optimization_barrier((*first, to_right, to_left))
        go_right, go_left = to_right[:, :cut] + first[0].astype(F32), to_left[:, cut:] + first[1].astype(F32)
        go_right, go_left, mine, other = lax.optimization_barrier(
            (go_right.astype(BF16), go_left.astype(BF16), mine, other)
        )
        first = right(go_right), left(go_left)
    (here,) = partial([0])
    *first, here = lax.optimization_barrier((*first, here))
    full_out = here + jnp.concatenate(
        [
            first[0].astype(F32) + second[1].astype(F32),
            second[0].astype(F32) + first[1].astype(F32),
        ],
        1,
    )

    own_peak, turned = lax.optimization_barrier((jnp.max(jnp.abs(full_out), axis=0), full_out.T))
    peak = peak_over(own_peak.reshape(steps, step_rows), n) + 1e-6
    quantized = (turned.reshape(steps, step_rows, width) / peak[:, :, None]).astype(BF16)
    return quantized, peak


def plain_layer(tokens_q, token_scale, weight_in, weight_out):
    steps, step_rows, width = tokens_q.shape
    rows = steps * step_rows
    tokens = lax.all_gather(tokens_q.reshape(rows, width), "hid", axis=1, tiled=True)
    partial_pre = jnp.dot(tokens, weight_in, preferred_element_type=F32) * token_scale.reshape(rows, 1)
    hidden = gelu(lax.psum(partial_pre, "mdl"))
    sums = lax.dot_general(weight_out, hidden, (((0,), (1,)), ((), ())), preferred_element_type=F32)
    columns = lax.psum_scatter(sums, "hid", scatter_dimension=0, tiled=True)
    full_out = columns.T.reshape(steps, step_rows, width)
    peak = lax.pmax(jnp.max(jnp.abs(full_out), axis=2), ("hid", "mdl")) + 1e-6
    return (full_out / peak[:, :, None]).astype(BF16), peak


def per_device(tokens_q, token_scale, weight_in, weight_out):
    n = lax.axis_size("hid")
    steps, step_rows, width = tokens_q.shape
    hidden_width = weight_in.shape[1]
    window = -(-width // 128) * 128
    ring = (
        n >= 4
        and n & (n - 1) == 0
        and lax.axis_size("mdl") == 2
        and width % 64 == 0
        and width > 128
        and window - width in (0, 64)
        and hidden_width % 256 == 0
        and weight_out.shape[1] == n * width
        and (steps * step_rows) % 32 == 0
    )
    layer = ring_layer if ring else plain_layer
    return layer(tokens_q, token_scale, weight_in, weight_out)


def solution(mesh):
    return jax.shard_map(
        per_device,
        mesh=mesh,
        in_specs=(
            P(None, "groups", ("mdl", "hid")),
            P(None, "groups"),
            P("mdl", "hid"),
            P("hid", "mdl"),
        ),
        out_specs=(P(None, "groups", ("mdl", "hid")), P(None, "groups")),
        check_vma=False,
    )
```

```python
import functools

import jax
import jax.numpy as jnp
from jax import lax
from jax.experimental import pallas as pl
from jax.experimental.pallas import tpu as pltpu
from jax.sharding import PartitionSpec as P

F32, BF16 = jnp.float32, jnp.bfloat16
ROWS = 256
SLOTS = 3


def divisor(size, most):
    best = 128
    for tile in range(128, most + 1, 128):
        if size % tile == 0:
            best = tile
    return best


def ring_order(n):
    return [2 * i for i in range(n // 2)] + [2 * i + 1 for i in reversed(range(n // 2))]


def ring_shard(n, offset):
    me = lax.axis_index("hid")
    place = jnp.where(lax.rem(me, 2) == 0, lax.div(me, 2), n - 1 - lax.div(me, 2))
    place = lax.rem(place + offset + n, n)
    return jnp.where(place < n // 2, 2 * place, 2 * (n - 1 - place) + 1)


def cost(rows, depth, columns, extra=0):
    return pl.CostEstimate(
        flops=2 * rows * depth * columns,
        bytes_accessed=2 * depth * columns + extra,
        transcendentals=0,
    )


def gather_matmul_kernel(n, offsets, block, cuts, counts, with_total, with_scale, in_place, *refs):
    pieces = len(counts)
    tokens, refs = refs[: sum(counts)], refs[sum(counts) :]
    weight, refs = refs[0], refs[1:]
    total, refs = (refs[0], refs[1:]) if with_total else (None, refs)
    scale, refs = (refs[0], refs[1:]) if with_scale else (None, refs)
    factors, refs = (refs[-1], refs[:-1]) if with_scale else (None, refs)
    out, stacked, turned, held, sems = refs
    depth, columns = pieces * block, weight.shape[1]
    shards = [ring_shard(n, offset) for offset in offsets]
    first = (1 - lax.axis_index("mdl")) * (columns // 2)

    def copies(at):
        low, size = cuts[at], cuts[at + 1] - cuts[at]
        return [
            pltpu.make_async_copy(
                weight.at[
                    pl.ds(pl.multiple_of(shards[piece] * block, 16), block),
                    pl.ds(pl.multiple_of(lax.rem(first + low, columns), 128), size),
                ],
                held.at[at % SLOTS, pl.ds(piece * block, block), pl.ds(0, size)],
                sems.at[at % SLOTS, piece],
            )
            for piece in range(pieces)
        ]

    for at in range(min(SLOTS, len(cuts)) - 1):
        for one in copies(at):
            one.start()
    index = 0
    for piece, count in enumerate(counts):
        lane = 0
        for ref in tokens[index : index + count]:
            stacked[piece * block : (piece + 1) * block, lane : lane + ref.shape[1]] = ref[...]
            lane += ref.shape[1]
        index += count
    if stacked.shape[0] > depth:
        stacked[depth:, :] = jnp.zeros((stacked.shape[0] - depth, stacked.shape[1]), BF16)
    turned[...] = stacked[...].T
    if with_scale:
        for index in range(factors.shape[0]):
            factors[index] = jnp.broadcast_to(scale[index : index + 1, :], (128, scale.shape[1])).T
    for at in range(len(cuts) - 1):
        if at + SLOTS < len(cuts):
            for one in copies(at + SLOTS - 1):
                one.start()
        for one in copies(at):
            one.wait()
        stride = turned.shape[0] // factors.shape[0] if with_scale else ROWS
        for top in range(0, turned.shape[0], stride):
            rows = slice(top, min(top + stride, turned.shape[0]))
            size = cuts[at + 1] - cuts[at]
            result = jnp.dot(turned[rows, :depth], held[at % SLOTS, :, :size], preferred_element_type=F32)
            if with_total:
                result = result + total[rows, cuts[at] : cuts[at + 1]]
            if with_scale:
                result = result * factors[top // stride][:, :1]
            low = cuts[at] if in_place else cuts[at] - cuts[0]
            out[rows, low : low + size] = result.astype(out.dtype)


def gather_matmul(n, offsets, chunks, weight, total=None, half=None, scale=None, dtype=F32):
    counts = tuple(len(chunk) for chunk in chunks)
    flat = [part for chunk in chunks for part in chunk]
    block, columns = flat[0].shape[0], weight.shape[1]
    rows = sum(part.shape[1] for part in chunks[0])
    depth = block * len(chunks)
    padded = -(-depth // 128) * 128
    tile = divisor(columns // 2, 768)
    vmem = pl.BlockSpec(memory_space=pltpu.VMEM)
    whole = scale is None
    low, high = {None: (0, columns), 0: (0, columns // 2), 1: (columns // 2, columns)}[half]
    cuts = tuple(range(low, high + 1, tile))
    if tile == 768:
        cuts = (low, low + 256, *cuts[1:])
    operands = flat + [weight] + [extra for extra in (total, scale) if extra is not None]
    in_specs = [vmem] * len(operands)
    in_specs[len(flat)] = pl.BlockSpec(memory_space=pl.ANY)
    return pl.pallas_call(
        functools.partial(
            gather_matmul_kernel, n, tuple(offsets), block, cuts, counts, total is not None, not whole, whole
        ),
        in_specs=in_specs,
        out_specs=vmem,
        scratch_shapes=[
            pltpu.VMEM((padded, rows), BF16),
            pltpu.VMEM((rows, padded), BF16),
            pltpu.VMEM((SLOTS, depth, tile), BF16),
            pltpu.SemaphoreType.DMA((SLOTS, len(chunks))),
        ]
        + ([] if whole else [pltpu.VMEM((scale.shape[0], scale.shape[1], 128), F32)]),
        out_shape=jax.ShapeDtypeStruct((rows, columns if whole else high - low), dtype),
        input_output_aliases={1 + len(flat): 0} if total is not None and whole else {},
        compiler_params=pltpu.CompilerParams(vmem_limit_bytes=14 << 20),
        cost_estimate=cost(rows, depth, high - low),
    )(*operands)


def block_matmul_kernel(n, offsets, width, window, depth, sides, with_start, *refs):
    blocks = len(offsets)
    hidden, refs = refs[: len(sides)], refs[len(sides) :]
    weight, refs = refs[0], refs[1:]
    starts, refs = (refs[:blocks], refs[blocks:]) if with_start else (None, refs)
    outs, refs = refs[:blocks], refs[blocks:]
    held, total, sems = refs
    core, (rows, half) = lax.axis_index("mdl"), hidden[0].shape
    columns = [ring_shard(n, offset) * width for offset in offsets]
    pieces = [(0, 0, depth), (0, depth, half)] + [(index, 0, half) for index in range(1, len(sides))]

    def copies(number):
        index, low, high = pieces[number]
        row = jnp.where(sides[index] == 0, core, 1 - core) * half + low
        return [
            pltpu.make_async_copy(
                weight.at[
                    pl.ds(pl.multiple_of(row, 128), high - low),
                    pl.ds(pl.multiple_of(lax.div(columns[block], 128) * 128, 128), window),
                ],
                held.at[pl.ds(index * half + low, high - low), pl.ds(block * window, window)],
                sems.at[number, block],
            )
            for block in range(blocks)
        ]

    for number in range(len(pieces)):
        for one in copies(number):
            one.start()
    for number, (index, low, high) in enumerate(pieces):
        for one in copies(number):
            one.wait()
        for top in range(0, rows, ROWS):
            here = slice(top, min(top + ROWS, rows))
            part = jnp.dot(
                hidden[index][here, low:high],
                held[index * half + low : index * half + high],
                preferred_element_type=F32,
            )
            if number > 0:
                part = total[here] + part
            if number + 1 < len(pieces):
                total[here] = part
                continue
            for block in range(blocks):
                span = pl.ds(pl.multiple_of(window - width - lax.rem(columns[block], 128), 16), window)
                value = part[:, block * window : (block + 1) * window].T
                if with_start:
                    value = value + starts[block][span, here]
                outs[block][span, here] = value.astype(outs[block].dtype)


def block_matmul(n, offsets, sides, hidden, weight, width, starts=None, dtype=F32):
    rows, half = hidden[0].shape
    window = -(-width // 128) * 128
    blocks, both = len(offsets), len(sides) * half
    depth = divisor(half, 768)
    vmem = pl.BlockSpec(memory_space=pltpu.VMEM)
    starts = [] if starts is None else starts
    return pl.pallas_call(
        functools.partial(block_matmul_kernel, n, tuple(offsets), width, window, depth, sides, bool(starts)),
        in_specs=[vmem] * len(sides) + [pl.BlockSpec(memory_space=pl.ANY)] + [vmem] * len(starts),
        out_specs=[vmem] * blocks,
        scratch_shapes=[
            pltpu.VMEM((both, blocks * window), BF16),
            pltpu.VMEM((rows, blocks * window), F32),
            pltpu.SemaphoreType.DMA((1 + len(sides), blocks)),
        ],
        out_shape=[jax.ShapeDtypeStruct((2 * window - width, rows), dtype)] * blocks,
        compiler_params=pltpu.CompilerParams(vmem_limit_bytes=22 << 20),
        cost_estimate=cost(rows, both, blocks * window),
    )(*hidden, weight, *starts)


def gelu(pre):
    return (0.5 * pre * (1.0 + lax.erf(pre * 0.7071067811865476))).astype(BF16)


def peak_over(value, n):
    value = jnp.maximum(value, lax.ppermute(value, "mdl", [(0, 1), (1, 0)]))
    near = [lax.ppermute(value, "hid", [(i, i ^ flip) for i in range(n)]) for flip in (1, 2, 3)]
    value = functools.reduce(jnp.maximum, near, value)
    reach = 4
    while reach < n:
        value = jnp.maximum(value, lax.ppermute(value, "hid", [(i, i ^ reach) for i in range(n)]))
        reach *= 2
    return value


def ring_layer(tokens_q, token_scale, weight_in, weight_out):
    n = lax.axis_size("hid")
    steps, step_rows, width = tokens_q.shape
    rows = steps * step_rows
    cut = rows // 2
    order = ring_order(n)
    rightward = [(order[i], order[(i + 1) % n]) for i in range(n)]
    leftward = [(b, a) for a, b in rightward]

    def right(value):
        return lax.ppermute(value, "hid", rightward)

    def left(value):
        return lax.ppermute(value, "hid", leftward)

    own = tokens_q.reshape(rows, width).T
    reach = n // 2

    def multiply(offsets, chunks, total, **kind):
        return gather_matmul(n, offsets, chunks, weight_in, total, **kind)

    first = right(own[:, :cut]), left(own[:, cut:])
    second = right(own[:, cut:]), left(own[:, :cut])
    total = multiply([0], [[own]], None)
    for hop in range(1, reach):
        *first, total = lax.optimization_barrier((*first, total))
        ahead = right(first[0]), left(first[1])
        *second, total = lax.optimization_barrier((*second, total))
        chunks, offsets = [[first[0], second[0]], [second[1], first[1]]], [-hop, hop]
        total = multiply(offsets, chunks, total, half=None if hop < reach - 1 else 0)
        if hop < reach - 1:
            second = right(second[0]), left(second[1])
        first = ahead
    *last, total = lax.optimization_barrier((*first, total))

    away = multiply([reach], [last], total, half=0, scale=token_scale, dtype=BF16)
    received = lax.ppermute(away, "mdl", [(0, 1), (1, 0)])
    kept = multiply([*offsets, reach], [*chunks, last], total, half=1, scale=token_scale)
    mine = gelu(kept + received.astype(F32))
    other = lax.ppermute(mine, "mdl", [(0, 1), (1, 0)])

    def partial(offsets, sides=(0, 1), **kind):
        hidden = [(mine, other)[side] for side in sides]
        return block_matmul(n, offsets, sides, hidden, weight_out, width, **kind)

    spare = -width % 128

    def part_of(value, lanes=slice(None)):
        return value[spare : spare + width, lanes]

    head, tail = slice(0, cut), slice(cut, rows)
    begun = partial([reach], sides=(0,))
    (far,) = partial([reach], sides=(1,), starts=begun, dtype=BF16)
    first = right(part_of(far, head)), left(part_of(far, tail))
    second = None
    for hop in range(reach - 1, 0, -1):
        to_right, to_left = partial([hop, -hop])
        if second is None:
            go_right, go_left = part_of(to_right, tail), part_of(to_left, head)
        else:
            *second, to_right, to_left = lax.optimization_barrier((*second, to_right, to_left))
            go_right = part_of(to_right, tail) + second[0].astype(F32)
            go_left = part_of(to_left, head) + second[1].astype(F32)
        go_right, go_left = lax.optimization_barrier((go_right.astype(BF16), go_left.astype(BF16)))
        second = right(go_right), left(go_left)
        *first, to_right, to_left = lax.optimization_barrier((*first, to_right, to_left))
        go_right = part_of(to_right, head) + first[0].astype(F32)
        go_left = part_of(to_left, tail) + first[1].astype(F32)
        go_right, go_left, mine, other = lax.optimization_barrier(
            (go_right.astype(BF16), go_left.astype(BF16), mine, other)
        )
        first = right(go_right), left(go_left)
    (here,) = partial([0])
    *first, here = lax.optimization_barrier((*first, here))
    full_out = part_of(here) + jnp.concatenate(
        [
            first[0].astype(F32) + second[1].astype(F32),
            second[0].astype(F32) + first[1].astype(F32),
        ],
        1,
    )

    own_peak, turned = lax.optimization_barrier((jnp.max(jnp.abs(full_out), axis=0), full_out.T))
    peak = peak_over(own_peak.reshape(steps, step_rows), n) + 1e-6
    quantized = (turned.reshape(steps, step_rows, width) / peak[:, :, None]).astype(BF16)
    return quantized, peak


def plain_layer(tokens_q, token_scale, weight_in, weight_out):
    steps, step_rows, width = tokens_q.shape
    rows = steps * step_rows
    tokens = lax.all_gather(tokens_q.reshape(rows, width), "hid", axis=1, tiled=True)
    partial_pre = jnp.dot(tokens, weight_in, preferred_element_type=F32) * token_scale.reshape(rows, 1)
    hidden = gelu(lax.psum(partial_pre, "mdl"))
    sums = lax.dot_general(weight_out, hidden, (((0,), (1,)), ((), ())), preferred_element_type=F32)
    columns = lax.psum_scatter(sums, "hid", scatter_dimension=0, tiled=True)
    full_out = columns.T.reshape(steps, step_rows, width)
    peak = lax.pmax(jnp.max(jnp.abs(full_out), axis=2), ("hid", "mdl")) + 1e-6
    return (full_out / peak[:, :, None]).astype(BF16), peak


def per_device(tokens_q, token_scale, weight_in, weight_out):
    n = lax.axis_size("hid")
    steps, step_rows, width = tokens_q.shape
    hidden_width = weight_in.shape[1]
    window = -(-width // 128) * 128
    ring = (
        n >= 4
        and n & (n - 1) == 0
        and lax.axis_size("mdl") == 2
        and width % 64 == 0
        and width > 128
        and window - width in (0, 64)
        and hidden_width % 256 == 0
        and weight_out.shape[1] == n * width
        and (steps * step_rows) % 32 == 0
    )
    layer = ring_layer if ring else plain_layer
    return layer(tokens_q, token_scale, weight_in, weight_out)


def solution(mesh):
    return jax.shard_map(
        per_device,
        mesh=mesh,
        in_specs=(
            P(None, "groups", ("mdl", "hid")),
            P(None, "groups"),
            P("mdl", "hid"),
            P("hid", "mdl"),
        ),
        out_specs=(P(None, "groups", ("mdl", "hid")), P(None, "groups")),
        check_vma=False,
    )
```

```python
import functools

import jax
import jax.numpy as jnp
from jax import lax
from jax.experimental import pallas as pl
from jax.experimental.pallas import tpu as pltpu
from jax.sharding import PartitionSpec as P

F32, BF16 = jnp.float32, jnp.bfloat16
ROWS = 256
SLOTS = 3


def divisor(size, most):
    best = 128
    for tile in range(128, most + 1, 128):
        if size % tile == 0:
            best = tile
    return best


def ring_order(n):
    return [2 * i for i in range(n // 2)] + [2 * i + 1 for i in reversed(range(n // 2))]


def ring_shard(n, offset):
    me = lax.axis_index("hid")
    place = jnp.where(lax.rem(me, 2) == 0, lax.div(me, 2), n - 1 - lax.div(me, 2))
    place = lax.rem(place + offset + n, n)
    return jnp.where(place < n // 2, 2 * place, 2 * (n - 1 - place) + 1)


def cost(rows, depth, columns, extra=0):
    return pl.CostEstimate(
        flops=2 * rows * depth * columns,
        bytes_accessed=2 * depth * columns + extra,
        transcendentals=0,
    )


def gather_matmul_kernel(n, offsets, block, cuts, counts, with_total, with_scale, in_place, *refs):
    pieces = len(counts)
    tokens, refs = refs[: sum(counts)], refs[sum(counts) :]
    weight, refs = refs[0], refs[1:]
    total, refs = (refs[0], refs[1:]) if with_total else (None, refs)
    scale, refs = (refs[0], refs[1:]) if with_scale else (None, refs)
    factors, refs = (refs[-1], refs[:-1]) if with_scale else (None, refs)
    out, stacked, turned, held, sems = refs
    depth, columns = pieces * block, weight.shape[1]
    shards = [ring_shard(n, offset) for offset in offsets]
    first = (1 - lax.axis_index("mdl")) * (columns // 2)

    def copies(at):
        low, size = cuts[at], cuts[at + 1] - cuts[at]
        return [
            pltpu.make_async_copy(
                weight.at[
                    pl.ds(pl.multiple_of(shards[piece] * block, 16), block),
                    pl.ds(pl.multiple_of(lax.rem(first + low, columns), 128), size),
                ],
                held.at[at % SLOTS, pl.ds(piece * block, block), pl.ds(0, size)],
                sems.at[at % SLOTS, piece],
            )
            for piece in range(pieces)
        ]

    for at in range(min(SLOTS, len(cuts)) - 1):
        for one in copies(at):
            one.start()
    index = 0
    for piece, count in enumerate(counts):
        lane = 0
        for ref in tokens[index : index + count]:
            stacked[piece * block : (piece + 1) * block, lane : lane + ref.shape[1]] = ref[...]
            lane += ref.shape[1]
        index += count
    if stacked.shape[0] > depth:
        stacked[depth:, :] = jnp.zeros((stacked.shape[0] - depth, stacked.shape[1]), BF16)
    turned[...] = stacked[...].T
    if with_scale:
        for index in range(factors.shape[0]):
            factors[index] = jnp.broadcast_to(scale[index : index + 1, :], (128, scale.shape[1])).T
    for at in range(len(cuts) - 1):
        if at + SLOTS < len(cuts):
            for one in copies(at + SLOTS - 1):
                one.start()
        for one in copies(at):
            one.wait()
        stride = turned.shape[0] // factors.shape[0] if with_scale else ROWS
        for top in range(0, turned.shape[0], stride):
            rows = slice(top, min(top + stride, turned.shape[0]))
            size = cuts[at + 1] - cuts[at]
            result = jnp.dot(turned[rows, :depth], held[at % SLOTS, :, :size], preferred_element_type=F32)
            if with_total:
                result = result + total[rows, cuts[at] : cuts[at + 1]]
            if with_scale:
                result = result * factors[top // stride][:, :1]
            low = cuts[at] if in_place else cuts[at] - cuts[0]
            out[rows, low : low + size] = result.astype(out.dtype)


def gather_matmul(n, offsets, chunks, weight, total=None, half=None, scale=None, dtype=F32):
    counts = tuple(len(chunk) for chunk in chunks)
    flat = [part for chunk in chunks for part in chunk]
    block, columns = flat[0].shape[0], weight.shape[1]
    rows = sum(part.shape[1] for part in chunks[0])
    depth = block * len(chunks)
    padded = -(-depth // 128) * 128
    tile = divisor(columns // 2, 768)
    vmem = pl.BlockSpec(memory_space=pltpu.VMEM)
    whole = scale is None
    low, high = {None: (0, columns), 0: (0, columns // 2), 1: (columns // 2, columns)}[half]
    cuts = tuple(range(low, high + 1, tile))
    if tile == 768:
        cuts = (low, low + 256, *cuts[1:])
    operands = flat + [weight] + [extra for extra in (total, scale) if extra is not None]
    in_specs = [vmem] * len(operands)
    in_specs[len(flat)] = pl.BlockSpec(memory_space=pl.ANY)
    return pl.pallas_call(
        functools.partial(
            gather_matmul_kernel, n, tuple(offsets), block, cuts, counts, total is not None, not whole, whole
        ),
        in_specs=in_specs,
        out_specs=vmem,
        scratch_shapes=[
            pltpu.VMEM((padded, rows), BF16),
            pltpu.VMEM((rows, padded), BF16),
            pltpu.VMEM((SLOTS, depth, tile), BF16),
            pltpu.SemaphoreType.DMA((SLOTS, len(chunks))),
        ]
        + ([] if whole else [pltpu.VMEM((scale.shape[0], scale.shape[1], 128), F32)]),
        out_shape=jax.ShapeDtypeStruct((rows, columns if whole else high - low), dtype),
        input_output_aliases={1 + len(flat): 0} if total is not None and whole else {},
        compiler_params=pltpu.CompilerParams(vmem_limit_bytes=14 << 20),
        cost_estimate=cost(rows, depth, high - low),
    )(*operands)


def block_matmul_kernel(n, offsets, width, window, depth, sides, with_start, *refs):
    blocks = len(offsets)
    hidden, refs = refs[: len(sides)], refs[len(sides) :]
    weight, refs = refs[0], refs[1:]
    starts, refs = (refs[:blocks], refs[blocks:]) if with_start else (None, refs)
    outs, refs = refs[:blocks], refs[blocks:]
    held, total, sems = refs
    core, (rows, half) = lax.axis_index("mdl"), hidden[0].shape
    columns = [ring_shard(n, offset) * width for offset in offsets]
    pieces = [(0, 0, depth), (0, depth, half)] + [(index, 0, half) for index in range(1, len(sides))]

    def copies(number):
        index, low, high = pieces[number]
        row = jnp.where(sides[index] == 0, core, 1 - core) * half + low
        return [
            pltpu.make_async_copy(
                weight.at[
                    pl.ds(pl.multiple_of(row, 128), high - low),
                    pl.ds(pl.multiple_of(lax.div(columns[block], 128) * 128, 128), window),
                ],
                held.at[pl.ds(index * half + low, high - low), pl.ds(block * window, window)],
                sems.at[number, block],
            )
            for block in range(blocks)
        ]

    for number in range(len(pieces)):
        for one in copies(number):
            one.start()
    for number, (index, low, high) in enumerate(pieces):
        for one in copies(number):
            one.wait()
        for top in range(0, rows, ROWS):
            here = slice(top, min(top + ROWS, rows))
            part = jnp.dot(
                hidden[index][here, low:high],
                held[index * half + low : index * half + high],
                preferred_element_type=F32,
            )
            if number > 0:
                part = total[here] + part
            if number + 1 < len(pieces):
                total[here] = part
                continue
            for block in range(blocks):
                span = pl.ds(pl.multiple_of(window - width - lax.rem(columns[block], 128), 16), window)
                value = part[:, block * window : (block + 1) * window].T
                if with_start:
                    value = value + starts[block][span, here]
                outs[block][span, here] = value.astype(outs[block].dtype)


def block_matmul(n, offsets, sides, hidden, weight, width, starts=None, dtype=F32):
    rows, half = hidden[0].shape
    window = -(-width // 128) * 128
    blocks, both = len(offsets), len(sides) * half
    depth = divisor(half, 768)
    vmem = pl.BlockSpec(memory_space=pltpu.VMEM)
    starts = [] if starts is None else starts
    return pl.pallas_call(
        functools.partial(block_matmul_kernel, n, tuple(offsets), width, window, depth, sides, bool(starts)),
        in_specs=[vmem] * len(sides) + [pl.BlockSpec(memory_space=pl.ANY)] + [vmem] * len(starts),
        out_specs=[vmem] * blocks,
        scratch_shapes=[
            pltpu.VMEM((both, blocks * window), BF16),
            pltpu.VMEM((rows, blocks * window), F32),
            pltpu.SemaphoreType.DMA((1 + len(sides), blocks)),
        ],
        out_shape=[jax.ShapeDtypeStruct((2 * window - width, rows), dtype)] * blocks,
        compiler_params=pltpu.CompilerParams(vmem_limit_bytes=22 << 20),
        cost_estimate=cost(rows, both, blocks * window),
    )(*hidden, weight, *starts)


def gelu(pre):
    return (0.5 * pre * (1.0 + lax.erf(pre * 0.7071067811865476))).astype(BF16)


def peak_over(value, n):
    def ask(flip, core):
        pairs = [(2 * i + c, 2 * (i ^ flip) + (c ^ core)) for i in range(n) for c in range(2)]
        return lax.ppermute(value, ("hid", "mdl"), pairs)

    far = [(0, 1)] + ([(4, 0), (4, 1)] if n > 4 else [])
    value = functools.reduce(jnp.maximum, [ask(*flips) for flips in far], value)
    value = functools.reduce(jnp.maximum, [ask(flip, 0) for flip in (1, 2, 3)], value)
    reach = 8
    while reach < n:
        value = jnp.maximum(value, ask(reach, 0))
        reach *= 2
    return value


def ring_layer(tokens_q, token_scale, weight_in, weight_out):
    n = lax.axis_size("hid")
    steps, step_rows, width = tokens_q.shape
    rows = steps * step_rows
    cut = rows // 2
    order = ring_order(n)
    rightward = [(order[i], order[(i + 1) % n]) for i in range(n)]
    leftward = [(b, a) for a, b in rightward]

    def right(value):
        return lax.ppermute(value, "hid", rightward)

    def left(value):
        return lax.ppermute(value, "hid", leftward)

    own = tokens_q.reshape(rows, width).T
    reach = n // 2

    def multiply(offsets, chunks, total, **kind):
        return gather_matmul(n, offsets, chunks, weight_in, total, **kind)

    first = right(own[:, :cut]), left(own[:, cut:])
    second = right(own[:, cut:]), left(own[:, :cut])
    total = multiply([0], [[own]], None)
    for hop in range(1, reach):
        *first, total = lax.optimization_barrier((*first, total))
        ahead = right(first[0]), left(first[1])
        *second, total = lax.optimization_barrier((*second, total))
        chunks, offsets = [[first[0], second[0]], [second[1], first[1]]], [-hop, hop]
        total = multiply(offsets, chunks, total, half=None if hop < reach - 1 else 0)
        if hop < reach - 1:
            second = right(second[0]), left(second[1])
        first = ahead
    *last, total = lax.optimization_barrier((*first, total))

    away = multiply([reach], [last], total, half=0, scale=token_scale, dtype=BF16)
    received = lax.ppermute(away, "mdl", [(0, 1), (1, 0)])
    kept = multiply([*offsets, reach], [*chunks, last], total, half=1, scale=token_scale)
    mine = gelu(kept + received.astype(F32))
    other = lax.ppermute(mine, "mdl", [(0, 1), (1, 0)])

    def partial(offsets, sides=(0, 1), **kind):
        hidden = [(mine, other)[side] for side in sides]
        return block_matmul(n, offsets, sides, hidden, weight_out, width, **kind)

    spare = -width % 128

    def part_of(value, lanes=slice(None)):
        return value[spare : spare + width, lanes]

    head, tail = slice(0, cut), slice(cut, rows)
    begun = partial([reach], sides=(0,))
    (far,) = partial([reach], sides=(1,), starts=begun, dtype=BF16)
    first = right(part_of(far, head)), left(part_of(far, tail))
    second = None
    for hop in range(reach - 1, 0, -1):
        to_right, to_left = partial([hop, -hop])
        if second is None:
            go_right, go_left = part_of(to_right, tail), part_of(to_left, head)
        else:
            *second, to_right, to_left = lax.optimization_barrier((*second, to_right, to_left))
            go_right = part_of(to_right, tail) + second[0].astype(F32)
            go_left = part_of(to_left, head) + second[1].astype(F32)
        go_right, go_left = lax.optimization_barrier((go_right.astype(BF16), go_left.astype(BF16)))
        second = right(go_right), left(go_left)
        *first, to_right, to_left = lax.optimization_barrier((*first, to_right, to_left))
        go_right = part_of(to_right, head) + first[0].astype(F32)
        go_left = part_of(to_left, tail) + first[1].astype(F32)
        go_right, go_left, mine, other = lax.optimization_barrier(
            (go_right.astype(BF16), go_left.astype(BF16), mine, other)
        )
        first = right(go_right), left(go_left)
    (here,) = partial([0])
    *first, here = lax.optimization_barrier((*first, here))
    full_out = part_of(here) + jnp.concatenate(
        [
            first[0].astype(F32) + second[1].astype(F32),
            second[0].astype(F32) + first[1].astype(F32),
        ],
        1,
    )

    own_peak, turned = lax.optimization_barrier((jnp.max(jnp.abs(full_out), axis=0), full_out.T))
    peak = peak_over(own_peak.reshape(steps, step_rows), n) + 1e-6
    quantized = (turned.reshape(steps, step_rows, width) / peak[:, :, None]).astype(BF16)
    return quantized, peak


def plain_layer(tokens_q, token_scale, weight_in, weight_out):
    steps, step_rows, width = tokens_q.shape
    rows = steps * step_rows
    tokens = lax.all_gather(tokens_q.reshape(rows, width), "hid", axis=1, tiled=True)
    partial_pre = jnp.dot(tokens, weight_in, preferred_element_type=F32) * token_scale.reshape(rows, 1)
    hidden = gelu(lax.psum(partial_pre, "mdl"))
    sums = lax.dot_general(weight_out, hidden, (((0,), (1,)), ((), ())), preferred_element_type=F32)
    columns = lax.psum_scatter(sums, "hid", scatter_dimension=0, tiled=True)
    full_out = columns.T.reshape(steps, step_rows, width)
    peak = lax.pmax(jnp.max(jnp.abs(full_out), axis=2), ("hid", "mdl")) + 1e-6
    return (full_out / peak[:, :, None]).astype(BF16), peak


def per_device(tokens_q, token_scale, weight_in, weight_out):
    n = lax.axis_size("hid")
    steps, step_rows, width = tokens_q.shape
    hidden_width = weight_in.shape[1]
    window = -(-width // 128) * 128
    ring = (
        n >= 4
        and n & (n - 1) == 0
        and lax.axis_size("mdl") == 2
        and width % 64 == 0
        and width > 128
        and window - width in (0, 64)
        and hidden_width % 256 == 0
        and weight_out.shape[1] == n * width
        and (steps * step_rows) % 32 == 0
    )
    layer = ring_layer if ring else plain_layer
    return layer(tokens_q, token_scale, weight_in, weight_out)


def solution(mesh):
    return jax.shard_map(
        per_device,
        mesh=mesh,
        in_specs=(
            P(None, "groups", ("mdl", "hid")),
            P(None, "groups"),
            P("mdl", "hid"),
            P("hid", "mdl"),
        ),
        out_specs=(P(None, "groups", ("mdl", "hid")), P(None, "groups")),
        check_vma=False,
    )
```
